256 devices in a mesh: lat: 64 (over x, z, y_hi), lon: 4 (over y_lo, core).
Axes of the slice: x: 4, y: 4 (y_hi: 2, y_lo: 2; y = y_hi * 2 + y_lo), z: 8, core: 2. Of those that a mesh axis runs over, the one named last changes fastest.
Arguments:
- inputs: bfloat16 [512, 1024, 512], P('lat', 'lon'), may hold values from -22 to 22
- cotangent: bfloat16 [512, 1024, 512], P('lat', 'lon'), may hold values from -16 to 16
- basis_values: float32 [512, 5, 9], replicated, may hold values from -0.6 to 0.6
- basis_index: int32 [512, 5, 9], replicated, may hold values from 0 to 8
- lon_reach: int32 [512, 5], replicated, may hold values from 1 to 4
- filters: float32 [512, 9], replicated, may hold values from -4 to 4
- weight_in: bfloat16 [512, 512], replicated, may hold values from -0.25 to 0.25
- weight_out: bfloat16 [512, 512], replicated, may hold values from -0.25 to 0.25
Outputs:
- output: bfloat16 [512, 1024, 512], P('lat', 'lon')
- grad_inputs: bfloat16 [512, 1024, 512], P('lat', 'lon')
- grad_weight_in: float32 [512, 512], P('lat')
- grad_weight_out: float32 [512, 512], P(None, 'lat')
- grad_filters: float32 [512, 9], P('lat')
The draws below stay inside these ranges and needn't reach their ends.
All inputs are finite; a program needn't handle non-finite values.
Results may differ from the reference program's by a relative error of at most 0.023.
Values may be sent and summed in bfloat16 or wider, within the bound.
No kernel may reach another device: no remote copies, remote signals or barrier semaphores. Data moves between devices by JAX's collectives and lax.ppermute only.
A program may use at most 128 MiB of HBM per device.

```python
import jax
import jax.numpy as jnp
from jax import lax

CH = 512
BASIS = 9
REACH_LAT = 2
REACH_LON = 4
LAT_DEV = 8
NLAT = 512
NLON = 1024
N_LAT = 64


def draw_inputs(key, part):
    key = jax.random.fold_in(key, 7)
    key_base, key_pair = jax.random.split(key, 2)
    band_count = NLAT // LAT_DEV
    base_noise = jnp.clip(jax.random.normal(key_base, (NLAT, NLON, CH), jnp.float32), -4.0, 4.0)
    pairing = jax.random.permutation(key_pair, band_count)
    row_band = jnp.arange(NLAT) // LAT_DEV
    chan_band = jnp.arange(CH) // (CH // band_count)
    spike_scale = jnp.where(pairing[row_band][:, None] == chan_band[None, :], 3.0, 1.0).astype(jnp.float32)
    chan_scale = 0.6 + 1.2 * jnp.arange(CH).astype(jnp.float32) / CH
    values = base_noise * spike_scale[:, None, :] * chan_scale[None, None, :]
    return values.astype(jnp.bfloat16)


def set_ends(values, rng, low, high):
    index_at = [jax.random.randint(jax.random.fold_in(rng, axis), (), 0, length) for axis, length in enumerate(values.shape)]
    main_axis = values.shape.index(max(values.shape))
    neighbour = index_at[:main_axis] + [(index_at[main_axis] + 1) % values.shape[main_axis]] + index_at[main_axis + 1:]
    return values.at[tuple(index_at)].set(low).at[tuple(neighbour)].set(high)


def with_spikes(values, stream_key, source, target, shards_of, factor):
    def block_of(axis_at):
        return (jnp.arange(values.shape[axis_at]) // (values.shape[axis_at] // shards_of)).reshape((-1,) + (1,) * (values.ndim - 1 - axis_at))

    near = jax.random.permutation(stream_key, shards_of)[block_of(target)]
    second = (block_of(target) + shards_of // 2) % shards_of
    return jnp.where((block_of(source) == near) | (block_of(source) == second), factor * values, values)


def shard_levels(key, dims, cuts, low, top_value):
    loudness, own = 1.0, jax.random.fold_in(key, 6)
    for position, shards_of in cuts:
        heights = jnp.exp(jax.random.uniform(jax.random.fold_in(own, position), (shards_of,), jnp.float32, low / len(cuts), top_value / len(cuts)))
        loudness = loudness * jnp.repeat(heights, dims[position] // shards_of).reshape([-1 if axis == position else 1 for axis in range(len(dims))])
    return loudness


def noise(own_key, extent, spread, reach, cuts=(), held_as=jnp.bfloat16):
    array = spread * jax.random.normal(own_key, extent, jnp.float32)
    if cuts:
        array = array * shard_levels(own_key, extent, cuts, -0.22, 0.18)
    return jnp.clip(array, -reach, reach).astype(held_as)


def bell_draw_with(stream_key, extent, scale, most, cuts, heavy, held_as=jnp.bfloat16):
    values = scale * jax.random.normal(stream_key, extent, jnp.float32)
    if cuts:
        values = values * shard_levels(stream_key, extent, cuts, -0.22, 0.18)
    return jnp.clip(with_spikes(values, jax.random.fold_in(stream_key, 3), *heavy), -most, most).astype(held_as)


def setup_inputs(seed: int = 0) -> dict:
    keys = jax.random.split(jax.random.key(seed), 9)
    return {
        "inputs": draw_inputs(jax.random.fold_in(keys[8], 71), 0),
        "cotangent": bell_draw_with(keys[1], (NLAT, NLON, CH), 1.0, 16.0, ((0, 64), (1, 4)), (0, 2, 64, 4.0)),
        "basis_values": noise(keys[2], (NLAT, 2 * REACH_LAT + 1, 2 * REACH_LON + 1), 0.15, 0.6, (), jnp.float32),
        "basis_index": set_ends(jax.random.randint(keys[3], (NLAT, 2 * REACH_LAT + 1, 2 * REACH_LON + 1), 0, BASIS), jax.random.fold_in(keys[3], 1), 0, BASIS - 1).astype(jnp.int32),
        "lon_reach": set_ends(jax.random.randint(keys[4], (NLAT, 2 * REACH_LAT + 1), 1, REACH_LON + 1), jax.random.fold_in(keys[4], 1), 1, REACH_LON).astype(jnp.int32),
        "filters": noise(keys[5], (CH, BASIS), 1.0, 4.0, (), jnp.float32),
        "weight_in": noise(keys[6], (CH, CH), CH ** -0.5, 0.25),
        "weight_out": noise(keys[7], (CH, CH), CH ** -0.5, 0.25),
    }


eps = 1e-06

def tap_tables(basis_values, basis_index, lon_reach, filters):
    lon_taps = jnp.arange(2 * REACH_LON + 1) - REACH_LON
    within = (jnp.abs(lon_taps)[None, None, :] <= lon_reach[:, :, None]).astype(jnp.float32)
    onehot = (basis_index[:, :, :, None] == jnp.arange(BASIS)[None, None, None, :]).astype(jnp.float32)
    tap_weights = onehot * (basis_values.astype(jnp.float32) * within)[:, :, :, None]
    coeffs = jnp.einsum('rabk,ck->rabc', tap_weights, filters.astype(jnp.float32))
    return (tap_weights, coeffs)

def forward_taps(coeffs, wrapped, row_count, col_count):
    result = jnp.zeros((row_count, col_count, coeffs.shape[-1]), jnp.float32)
    for row_tap in range(2 * REACH_LAT + 1):
        for col_tap in range(2 * REACH_LON + 1):
            piece = wrapped[row_tap:row_tap + row_count, col_tap:col_tap + col_count].astype(jnp.float32)
            result = result + coeffs[:, row_tap, col_tap][:, None, :] * piece
    return result

def adjoint_taps(coeffs_ext, wrapped, row_count, col_count):
    result = jnp.zeros((row_count, col_count, coeffs_ext.shape[-1]), jnp.float32)
    for row_tap in range(2 * REACH_LAT + 1):
        row_first = 2 * REACH_LAT - row_tap
        for col_tap in range(2 * REACH_LON + 1):
            col_first = 2 * REACH_LON - col_tap
            piece = wrapped[row_first:row_first + row_count, col_first:col_first + col_count].astype(jnp.float32)
            result = result + coeffs_ext[row_first:row_first + row_count, row_tap, col_tap][:, None, :] * piece
    return result

def tap_products(wrapped, grad_filtered, row_count, col_count):
    cotan = grad_filtered.astype(jnp.float32)
    pieces = []
    for row_tap in range(2 * REACH_LAT + 1):
        for col_tap in range(2 * REACH_LON + 1):
            piece = wrapped[row_tap:row_tap + row_count, col_tap:col_tap + col_count].astype(jnp.float32)
            pieces.append(lax.optimization_barrier(jnp.sum(piece * cotan, axis=1)))
    stacked = jnp.stack(pieces, axis=1)
    return stacked.reshape(row_count, 2 * REACH_LAT + 1, 2 * REACH_LON + 1, cotan.shape[-1])

def mixer_pass(input_rows, filtered, cot_rows, weight_in, weight_out):
    shape = filtered.shape
    chans = shape[-1]
    low = filtered.astype(jnp.bfloat16).reshape(-1, chans)
    hidden = jnp.dot(low, weight_in, preferred_element_type=jnp.float32)
    activated, gelu_back = jax.vjp(jax.nn.gelu, hidden)
    act_low = activated.astype(jnp.bfloat16)
    mixed_out = jnp.dot(act_low, weight_out, preferred_element_type=jnp.float32)
    output = (input_rows.astype(jnp.float32).reshape(-1, chans) + mixed_out).astype(jnp.bfloat16).reshape(shape)
    cot_flat = cot_rows.reshape(-1, chans)
    grad_out = jnp.dot(act_low.T, cot_flat, preferred_element_type=jnp.float32)
    grad_act = jnp.dot(cot_flat, weight_out.T, preferred_element_type=jnp.float32)
    grad_hidden = gelu_back(grad_act)[0].astype(jnp.bfloat16)
    grad_in = jnp.dot(low.T, grad_hidden, preferred_element_type=jnp.float32)
    grad_filtered = jnp.dot(grad_hidden, weight_in.T, preferred_element_type=jnp.float32).astype(jnp.bfloat16).reshape(shape)
    return (output, grad_filtered, grad_in, grad_out)

def wrap_cycle(row_block):
    return jnp.concatenate([row_block[:, -REACH_LON:], row_block, row_block[:, :REACH_LON]], axis=1)

def reference(inputs, cotangent, basis_values, basis_index, lon_reach, filters, weight_in, weight_out):
    tap_weights, coeffs = tap_tables(basis_values, basis_index, lon_reach, filters)
    span = LAT_DEV + 2 * REACH_LAT
    padded = jnp.pad(inputs, ((REACH_LAT, REACH_LAT), (0, 0), (0, 0)))

    def first_pass(sums, block_index):
        first_row = (block_index * LAT_DEV).astype(jnp.int32)
        wrapped = wrap_cycle(lax.dynamic_slice_in_dim(padded, first_row, span, 0))
        coeff_rows = lax.dynamic_slice_in_dim(coeffs, first_row, LAT_DEV, 0)
        weight_rows = lax.dynamic_slice_in_dim(tap_weights, first_row, LAT_DEV, 0)
        input_rows = lax.dynamic_slice_in_dim(inputs, first_row, LAT_DEV, 0)
        cot_rows = lax.dynamic_slice_in_dim(cotangent, first_row, LAT_DEV, 0)
        filtered = forward_taps(coeff_rows, wrapped, LAT_DEV, NLON)
        output, grad_filtered, grad_in, grad_out = mixer_pass(input_rows, filtered, cot_rows, weight_in, weight_out)
        grad_filt = jnp.einsum('rabk,rabc->ck', weight_rows, tap_products(wrapped, grad_filtered, LAT_DEV, NLON))
        updated = (sums[0] + grad_in, sums[1] + grad_out, sums[2] + grad_filt)
        return (updated, (output, grad_filtered))
    zeros_init = (jnp.zeros((CH, CH), jnp.float32), jnp.zeros((CH, CH), jnp.float32), jnp.zeros((CH, BASIS), jnp.float32))
    sums, stacked = lax.scan(first_pass, zeros_init, jnp.arange(N_LAT))
    outputs = stacked[0].reshape(NLAT, NLON, CH)
    grad_field = stacked[1].reshape(NLAT, NLON, CH)
    grad_padded = jnp.pad(grad_field, ((REACH_LAT, REACH_LAT), (0, 0), (0, 0)))
    coeff_padded = jnp.pad(coeffs, ((REACH_LAT, REACH_LAT), (0, 0), (0, 0), (0, 0)))

    def second_pass(unused, block_index):
        first_row = (block_index * LAT_DEV).astype(jnp.int32)
        wrapped = wrap_cycle(lax.dynamic_slice_in_dim(grad_padded, first_row, span, 0))
        coeff_ext = lax.dynamic_slice_in_dim(coeff_padded, first_row, span, 0)
        cot_rows = lax.dynamic_slice_in_dim(cotangent, first_row, LAT_DEV, 0)
        back = adjoint_taps(coeff_ext, wrapped, LAT_DEV, NLON)
        return (unused, (cot_rows.astype(jnp.float32) + back).astype(jnp.bfloat16))
    unused, grad_rows = lax.scan(second_pass, jnp.zeros((), jnp.float32), jnp.arange(N_LAT))
    grad_inputs = grad_rows.reshape(NLAT, NLON, CH)
    grad_total = jnp.sum(sums[0] * sums[0]) + jnp.sum(sums[1] * sums[1]) + jnp.sum(sums[2] * sums[2])
    clip_scale = jnp.minimum(jnp.float32(1.0), jnp.float32(CH) / jnp.sqrt(grad_total + eps))
    return (outputs, grad_inputs, clip_scale * sums[0], clip_scale * sums[1], clip_scale * sums[2])
```

```python
import functools
import math

import jax
import jax.numpy as jnp
import numpy as np
from jax import lax
from jax.experimental import pallas as pl
from jax.experimental.pallas import tpu as pltpu
from jax.sharding import PartitionSpec as P

BASIS = 9
REACH_LAT = 2
REACH_LON = 4
ROW_TAPS = 2 * REACH_LAT + 1
COL_TAPS = 2 * REACH_LON + 1
PAIR = 2
WIN = PAIR + 2 * REACH_LAT
TILE = 16
HALF = TILE // 2
SPAN = 2 * TILE
CLIP = 512.0
EPS = 1e-06
BF = jnp.bfloat16
F32 = jnp.float32
VMEM_LIMIT = 56 * 1024 * 1024


def column_offsets():
    w = np.arange(SPAN)
    return np.where(w < HALF, w + TILE, w - TILE)


def band_constants(pairs):
    off = column_offsets()
    b = np.arange(COL_TAPS)[:, None, None]
    j = np.arange(TILE)[None, :, None]
    fwd = off[None, None, :] == j + b - REACH_LON
    adj = off[None, None, :] == j - b + REACH_LON
    ext = PAIR * pairs + 2 * REACH_LAT
    shape = (pairs, PAIR, WIN, ext, ROW_TAPS)
    pick_f, pick_a = np.zeros(shape), np.zeros(shape)
    for p in range(pairs):
        for r in range(PAIR):
            for a in range(WIN):
                if 0 <= a - r < ROW_TAPS:
                    pick_f[p, r, a, PAIR * p + r + REACH_LAT, a - r] = 1
                    pick_a[p, r, a, PAIR * p + a, r - a + 2 * REACH_LAT] = 1
    return fwd, adj, pick_f, pick_a


def band_matrices(tap_weights, pairs):
    fwd, adj, pick_f, pick_a = band_constants(pairs)
    taps = tap_weights.astype(BF)
    ext = taps.shape[0]
    pick = jnp.asarray(np.stack([pick_f, pick_a]).reshape(-1, ext * ROW_TAPS), BF)
    rows = jnp.dot(pick, taps.reshape(ext * ROW_TAPS, -1), preferred_element_type=F32).astype(BF)
    rows = rows.reshape(2, pairs, PAIR, WIN, COL_TAPS, BASIS)
    out = []
    for which, band in enumerate((fwd, adj)):
        full = jnp.einsum(
            "prabk,bjw->pkrjaw", rows[which], jnp.asarray(band, BF), preferred_element_type=F32
        )
        out.append(full.astype(BF).reshape(pairs, BASIS * PAIR * TILE, WIN * SPAN))
    return out


def dot(a, b, ca, cb):
    return lax.dot_general(a, b, (((ca,), (cb,)), ((), ())), preferred_element_type=F32)


def window(rows, sides, m, tiles):
    parts = []
    for row, side in zip(rows, sides):
        if m + 1 < tiles:
            right = row[(m + 1) * TILE : (m + 2) * TILE, :].astype(F32)[:HALF]
        else:
            right = side[...].astype(F32)[:HALF]
        if m > 0:
            left = row[(m - 1) * TILE : m * TILE, :].astype(F32)[HALF:]
        else:
            left = side[...].astype(F32)[HALF:]
        parts.append(jnp.concatenate([right, left], axis=0).astype(BF))
        parts.append(row[m * TILE : (m + 1) * TILE, :])
    return jnp.concatenate(parts, axis=0)


def mixer_body(
    rows, sides, band, filt, w_in, w_out, cot, out, gf, edge, gin, gout, gfilt, prev,
    y, low, hid, gact, act, gh,
):
    cols, chans = cot.shape[1:]
    tiles = cols // TILE
    cells = PAIR * cols
    for m in range(tiles):
        full = jnp.dot(band[0], window(rows, sides, m, tiles), preferred_element_type=F32)
        for r in range(PAIR):
            at = pl.ds(r * cols + m * TILE, TILE)
            total = None
            for k in range(BASIS):
                first = (k * PAIR + r) * TILE
                piece = full[first : first + TILE]
                y[k, at, :] = piece
                term = filt[k : k + 1, :] * piece
                total = term if total is None else total + term
            low[at, :] = total.astype(BF)
    cot_flat = cot[...].reshape(cells, chans)
    hid[...] = dot(low[...], w_in[...], 1, 0)
    gact[...] = dot(cot_flat, w_out[...], 1, 1)
    root = math.sqrt(2.0 / math.pi)
    step = 2 * TILE

    def pointwise(n, carry):
        at = pl.ds(pl.multiple_of(n * step, step), step)
        v = hid[at, :]
        sq = v * v
        t = jnp.tanh(v * (root + (root * 0.044715) * sq))
        half = 0.5 + 0.5 * t
        act[at, :] = (v * half).astype(BF)
        slope = half + (0.5 * v) * (1.0 - t * t) * (root + (3 * root * 0.044715) * sq)
        gh[at, :] = (gact[at, :] * slope).astype(BF)
        return carry

    lax.fori_loop(0, cells // step, pointwise, 0)
    mixed = dot(act[...], w_out[...], 1, 0)
    back = dot(gh[...], w_in[...], 1, 1)
    for r in range(PAIR):
        part = slice(r * cols, (r + 1) * cols)
        out[r] = (rows[REACH_LAT + r][...].astype(F32) + mixed[part]).astype(BF)
        gf[r] = back[part].astype(BF)
        edge[r] = jnp.concatenate(
            [back[r * cols : r * cols + HALF], back[(r + 1) * cols - HALF : (r + 1) * cols]], axis=0
        ).astype(BF)
    more_out = dot(cot_flat, act[...], 0, 0)
    more_in = dot(low[...], gh[...], 0, 0)
    if prev is None:
        first = pl.program_id(0) == 0

        @pl.when(first)
        def _():
            gin[...] = more_in
            gout[...] = more_out
            gfilt[...] = jnp.zeros_like(gfilt)

        @pl.when(jnp.logical_not(first))
        def _():
            gin[...] += more_in
            gout[...] += more_out

    else:
        gin[...] = prev[0][...] + more_in
        gout[...] = prev[1][...] + more_out
        gfilt[...] = prev[2][...]
    lanes = 128
    for c in range(chans // lanes):
        at_c = pl.ds(c * lanes, lanes)

        def correlate(n, sums, at_c=at_c):
            for r in range(PAIR):
                g = gf[r, pl.ds(pl.multiple_of(n * TILE, TILE), TILE), at_c].astype(F32)
                cell = pl.ds(pl.multiple_of(r * cols + n * TILE, TILE), TILE)
                new = []
                for k in range(BASIS):
                    prod = g * y[k, cell, at_c]
                    new.append(sums[k] + (prod[:8] + prod[8:]))
                sums = tuple(new)
            return sums

        zero = tuple(jnp.zeros((8, lanes), F32) for _ in range(BASIS))
        sums = lax.fori_loop(0, tiles, correlate, zero)
        for k in range(BASIS):
            gfilt[8 * k : 8 * k + 8, at_c] += sums[k]


def inner_kernel(x, side, band, filt, w_in, w_out, cot, out, gf, edge, gin, gout, gfilt, *scratch):
    i = pl.program_id(0)
    rows = [x.at[PAIR * i + a] for a in range(WIN)]
    sides = [side.at[PAIR * i + a] for a in range(WIN)]
    mixer_body(
        rows, sides, band, filt, w_in, w_out, cot, out, gf, edge, gin, gout, gfilt, None, *scratch
    )


def outer_kernel(
    low_end, x, side, halo, halo_side, band, filt, w_in, w_out, cot, keep, gin0, gout0, gfilt0,
    out, gf, edge, gin, gout, gfilt, *scratch,
):
    near = range(WIN - REACH_LAT)
    far = range(REACH_LAT)
    rows, sides = [x.at[a] for a in near], [side.at[a] for a in near]
    more_rows, more_sides = [halo.at[a] for a in far], [halo_side.at[a] for a in far]
    if low_end:
        rows, sides = more_rows + rows, more_sides + sides
    else:
        rows, sides = rows + more_rows, sides + more_sides
    mixer_body(
        rows, sides, band, filt, w_in, w_out, cot, out, gf, edge, gin, gout, gfilt,
        (gin0, gout0, gfilt0), *scratch,
    )


def adjoint_body(rows, sides, band, filt, cot, out):
    cols = cot.shape[1]
    tiles = cols // TILE
    for m in range(tiles):
        full = jnp.dot(band[0], window(rows, sides, m, tiles), preferred_element_type=F32)
        at = slice(m * TILE, (m + 1) * TILE)
        for r in range(PAIR):
            total = cot[r, at, :].astype(F32)
            for k in range(BASIS):
                first = (k * PAIR + r) * TILE
                total = total + filt[k : k + 1, :] * full[first : first + TILE]
            out[r, at, :] = total.astype(BF)


def inner_adjoint(top, mid, bottom, side, band, filt, cot, out):
    i = pl.program_id(0)
    for step in range(2):

        @pl.when(i == step)
        def _(step=step):
            every = [top.at[0], top.at[1]] + [mid.at[a] for a in range(4)]
            every = every + [bottom.at[0], bottom.at[1]]
            rows = every[PAIR * step : PAIR * step + WIN]
            sides = [side.at[PAIR * step + a] for a in range(WIN)]
            adjoint_body(rows, sides, band, filt, cot, out)


def outer_adjoint(low_end, end, mid, side, halo, halo_side, band, filt, cot, keep, out):
    far = range(REACH_LAT)
    more_rows, more_sides = [halo.at[a] for a in far], [halo_side.at[a] for a in far]
    own_sides = [side.at[a] for a in range(WIN - REACH_LAT)]
    if low_end:
        rows = more_rows + [end.at[a] for a in far] + [mid.at[a] for a in far]
        sides = more_sides + own_sides
    else:
        rows = [mid.at[a] for a in far] + [end.at[a] for a in far] + more_rows
        sides = own_sides + more_sides
    adjoint_body(rows, sides, band, filt, cot, out)


def whole(shape):
    return pl.BlockSpec(shape, lambda i: (0,) * len(shape))


def pair_block(shape, first):
    return pl.BlockSpec((PAIR,) + shape[1:], lambda i: (first + i,) + (0,) * (len(shape) - 1))


def params():
    return pltpu.CompilerParams(vmem_limit_bytes=VMEM_LIMIT)


def mixer_scratch(cols, chans):
    cells = PAIR * cols
    return [
        pltpu.VMEM((BASIS, cells, chans), F32),
        pltpu.VMEM((cells, chans), BF),
        pltpu.VMEM((cells, chans), F32),
        pltpu.VMEM((cells, chans), F32),
        pltpu.VMEM((cells, chans), BF),
        pltpu.VMEM((cells, chans), BF),
    ]


def mixer_outs(n, cols, chans):
    shapes = (
        jax.ShapeDtypeStruct((n * PAIR, cols, chans), BF),
        jax.ShapeDtypeStruct((n * PAIR, TILE, chans), BF),
        jax.ShapeDtypeStruct((chans, chans), F32),
        jax.ShapeDtypeStruct((chans, chans), F32),
        jax.ShapeDtypeStruct((8 * BASIS, chans), F32),
    )
    specs = [
        pair_block(shapes[0].shape, 0),
        pair_block(shapes[1].shape, 0),
        whole((chans, chans)),
        whole((chans, chans)),
        whole((8 * BASIS, chans)),
    ]
    return shapes, specs


def mixer_cost(n, cols, chans):
    cells = n * PAIR * cols
    flops = 2 * cells * chans * (6 * chans + BASIS * WIN * SPAN)
    return pl.CostEstimate(
        flops=flops, bytes_accessed=10 * cells * chans, transcendentals=cells * chans
    )


def mixer_inner(x, side, band, filt, w_in, w_out, cot):
    rows, cols, chans = x.shape
    shapes, specs = mixer_outs(2, cols, chans)
    return pl.pallas_call(
        inner_kernel,
        grid=(2,),
        in_specs=[
            whole(x.shape), whole(side.shape),
            pl.BlockSpec((1,) + band.shape[1:], lambda i: (1 + i, 0, 0)),
            whole(filt.shape), whole(w_in.shape), whole(w_out.shape), pair_block(cot.shape, 1),
        ],
        out_specs=[pair_block(x.shape, 1)] + specs,
        out_shape=(jax.ShapeDtypeStruct(x.shape, BF),) + shapes,
        scratch_shapes=mixer_scratch(cols, chans),
        compiler_params=params(),
        cost_estimate=mixer_cost(2, cols, chans),
        name="mixer_inner",
    )(x, side, band, filt, w_in, w_out, cot)


def mixer_outer(low_end, x, side, halo, halo_side, band, filt, w_in, w_out, cot, keep, sums):
    rows, cols, chans = x.shape
    pair = 0 if low_end else rows // PAIR - 1
    near = WIN - REACH_LAT
    at = 0 if low_end else rows // near - 1
    shapes, specs = mixer_outs(1, cols, chans)
    return pl.pallas_call(
        functools.partial(outer_kernel, low_end),
        grid=(1,),
        in_specs=[
            pl.BlockSpec((near, cols, chans), lambda i: (at, 0, 0)),
            pl.BlockSpec((near, TILE, chans), lambda i: (at, 0, 0)),
            whole(halo.shape), whole(halo_side.shape),
            pl.BlockSpec((1,) + band.shape[1:], lambda i: (pair, 0, 0)),
            whole(filt.shape), whole(w_in.shape), whole(w_out.shape), pair_block(cot.shape, pair),
            pl.BlockSpec(memory_space=pl.ANY),
        ] + [whole(s.shape) for s in sums],
        out_specs=[pair_block(x.shape, pair)] + specs,
        out_shape=(jax.ShapeDtypeStruct(x.shape, BF),) + shapes,
        scratch_shapes=mixer_scratch(cols, chans),
        input_output_aliases={9: 0, 10: 3, 11: 4, 12: 5},
        compiler_params=params(),
        cost_estimate=mixer_cost(1, cols, chans),
        name="mixer_low" if low_end else "mixer_high",
    )(x, side, halo, halo_side, band, filt, w_in, w_out, cot, keep, *sums)


def adjoint_cost(n, cols, chans):
    cells = n * PAIR * cols
    return pl.CostEstimate(
        flops=2 * cells * chans * BASIS * WIN * SPAN, bytes_accessed=6 * cells * chans,
        transcendentals=0,
    )


def adjoint_inner(top, mid, bottom, side, band, filt, cot):
    rows, cols, chans = cot.shape
    return pl.pallas_call(
        inner_adjoint,
        grid=(2,),
        in_specs=[
            whole(top.shape), whole(mid.shape), whole(bottom.shape), whole(side.shape),
            pl.BlockSpec((1,) + band.shape[1:], lambda i: (1 + i, 0, 0)),
            whole(filt.shape), pair_block(cot.shape, 1),
        ],
        out_specs=pair_block(cot.shape, 1),
        out_shape=jax.ShapeDtypeStruct(cot.shape, BF),
        compiler_params=params(),
        cost_estimate=adjoint_cost(2, cols, chans),
        name="adjoint_inner",
    )(top, mid, bottom, side, band, filt, cot)


def adjoint_outer(low_end, end, mid, side, halo, halo_side, band, filt, cot, keep):
    rows, cols, chans = cot.shape
    pair = 0 if low_end else rows // PAIR - 1
    near = WIN - REACH_LAT
    at = 0 if low_end else rows // near - 1
    return pl.pallas_call(
        functools.partial(outer_adjoint, low_end),
        grid=(1,),
        in_specs=[
            whole(end.shape),
            pl.BlockSpec((REACH_LAT, cols, chans), lambda i: (0 if low_end else 1, 0, 0)),
            pl.BlockSpec((near, TILE, chans), lambda i: (at, 0, 0)),
            whole(halo.shape), whole(halo_side.shape),
            pl.BlockSpec((1,) + band.shape[1:], lambda i: (pair, 0, 0)),
            whole(filt.shape), pair_block(cot.shape, pair),
            pl.BlockSpec(memory_space=pl.ANY),
        ],
        out_specs=pair_block(cot.shape, pair),
        out_shape=jax.ShapeDtypeStruct(cot.shape, BF),
        input_output_aliases={8: 0},
        compiler_params=params(),
        cost_estimate=adjoint_cost(1, cols, chans),
        name="adjoint_low" if low_end else "adjoint_high",
    )(end, mid, side, halo, halo_side, band, filt, cot, keep)


def exchange_columns(first, last):
    count = lax.axis_size("lon")
    up = [(i, (i + 1) % count) for i in range(count)]
    down = [(i, (i - 1) % count) for i in range(count)]
    right = lax.ppermute(first, "lon", down)
    left = lax.ppermute(last, "lon", up)
    return jnp.concatenate([right, left], axis=1)


def to_next(a):
    return lax.ppermute(a, "lat", [(i, i + 1) for i in range(lax.axis_size("lat") - 1)])


def to_last(a):
    return lax.ppermute(a, "lat", [(i + 1, i) for i in range(lax.axis_size("lat") - 1)])


def swap(a, bit):
    count = lax.axis_size("lon")
    return lax.ppermute(a, "lon", [(i, i ^ bit) for i in range(count)])


def reduce_grads(sums, chans):
    bands = lax.axis_size("lat")
    here = lax.axis_index("lon")
    per = chans // bands
    lanes = 128
    gin, gout, gfilt = sums
    filt = gfilt.reshape(BASIS, 8, bands, per).sum(1).transpose(1, 0, 2).reshape(bands, 1, -1)
    beside = jnp.broadcast_to(jnp.pad(filt, ((0, 0), (0, 0), (0, lanes - BASIS * per))), (bands, per, lanes))
    full_in = jnp.concatenate([gin.reshape(bands, per, chans), beside], axis=2)
    full_out = jnp.concatenate([gout.reshape(bands, per, chans), beside], axis=2)
    odd = here % 2 == 1
    keep = jnp.where(odd, full_out, full_in)
    give = jnp.where(odd, full_in, full_out).astype(BF)
    total = keep + swap(give, 1).astype(F32)
    upper = here // 2 == 1
    half = per // 2
    keep = jnp.where(upper, total[:, half:], total[:, :half])
    give = jnp.where(upper, total[:, :half], total[:, half:]).astype(BF)
    part = (keep + swap(give, 2).astype(F32)).astype(BF)
    share = jnp.sum(lax.all_to_all(part, "lat", 0, 0).astype(F32), axis=0)
    mats, filt_row = share[:, :chans], share[:1, chans : chans + BASIS * per]
    count = lax.axis_size("lon")
    square = jnp.sum(mats * mats) + jnp.sum(filt_row * filt_row) / count
    devices = bands * count
    spread = jnp.broadcast_to(square, (devices, 1, lanes))
    every = lax.all_to_all(spread, ("lat", "lon"), 0, 0)
    grad_total = jnp.sum(every[:, 0, 0])
    scale = jnp.minimum(jnp.float32(1.0), jnp.float32(CLIP) / jnp.sqrt(grad_total + EPS))
    other = swap(mats, 2)
    rows = jnp.concatenate(
        [jnp.where(upper, other, mats), jnp.where(upper, mats, other)], axis=0
    )
    across = swap(rows, 1)
    share_in = jnp.where(odd, across, rows)
    share_out = jnp.where(odd, rows, across)
    return (
        scale * share_in,
        (scale * share_out).T,
        scale * filt_row.reshape(BASIS, per).T,
    )


def local(inputs, cotangent, basis_values, basis_index, lon_reach, filters, weight_in, weight_out):
    rows, cols, chans = inputs.shape
    pairs = rows // PAIR
    band_at = lax.axis_index("lat")
    first_row = band_at * rows
    ext = rows + 2 * REACH_LAT
    with jax.named_scope("input_halo"):
        lo = to_next(inputs[rows - REACH_LAT :])
        hi = to_last(inputs[:REACH_LAT])
        side = exchange_columns(inputs[:, :HALF], inputs[:, cols - HALF :])
        lo_side = to_next(side[rows - REACH_LAT :])
        hi_side = to_last(side[:REACH_LAT])
    with jax.named_scope("bands"):
        lat_pad = (REACH_LAT, REACH_LAT)

        def cut(a):
            padded = jnp.pad(a, (lat_pad,) + ((0, 0),) * (a.ndim - 1))
            return lax.dynamic_slice_in_dim(padded, first_row, ext, 0)

        values, index, reach = cut(basis_values), cut(basis_index), cut(lon_reach)
        lon_taps = jnp.abs(jnp.arange(COL_TAPS) - REACH_LON)
        within = lon_taps[None, None, :] <= reach[:, :, None]
        onehot = index[:, :, :, None] == jnp.arange(BASIS)
        taps = jnp.where(onehot & within[..., None], values[..., None], 0.0)
        band, band_adj = band_matrices(taps, pairs)
        filt = jnp.pad(filters.T, ((0, 16 - BASIS), (0, 0)))
    out, gf_mid, edge_mid, *sums = mixer_inner(
        inputs, side, band, filt, weight_in, weight_out, cotangent
    )
    out, gf_lo, edge_lo, *sums = mixer_outer(
        True, inputs, side, lo, lo_side, band, filt, weight_in, weight_out, cotangent, out, sums
    )
    gf_up = to_last(gf_lo)
    out, gf_hi, edge_hi, *sums = mixer_outer(
        False, inputs, side, hi, hi_side, band, filt, weight_in, weight_out, cotangent, out, sums
    )
    with jax.named_scope("grad_halo"):
        gf_down = to_next(gf_hi)
        edge = jnp.concatenate([edge_lo, edge_mid, edge_hi], axis=0)
        gside = exchange_columns(edge[:, :HALF], edge[:, HALF:])
        glo_side = to_next(gside[rows - REACH_LAT :])
        ghi_side = to_last(gside[:REACH_LAT])
    back = adjoint_inner(gf_lo, gf_mid, gf_hi, gside, band_adj, filt, cotangent)
    shares = reduce_grads(sums, chans)
    back = adjoint_outer(
        True, gf_lo, gf_mid, gside, gf_down, glo_side, band_adj, filt, cotangent, back
    )
    back = adjoint_outer(
        False, gf_hi, gf_mid, gside, gf_up, ghi_side, band_adj, filt, cotangent, back
    )
    return (out, back) + shares


def solution(mesh):
    placed = (P("lat", "lon", None), P("lat", "lon", None), P(), P(), P(), P(), P(), P())
    return jax.shard_map(
        local,
        mesh=mesh,
        in_specs=placed,
        out_specs=(
            P("lat", "lon", None),
            P("lat", "lon", None),
            P("lat", None),
            P(None, "lat"),
            P("lat", None),
        ),
        check_vma=False,
    )
```

```python
import functools
import math

import jax
import jax.numpy as jnp
import numpy as np
from jax import lax
from jax.experimental import pallas as pl
from jax.experimental.pallas import tpu as pltpu
from jax.sharding import PartitionSpec as P

BASIS = 9
REACH_LAT = 2
REACH_LON = 4
ROW_TAPS = 2 * REACH_LAT + 1
COL_TAPS = 2 * REACH_LON + 1
PAIR = 2
WIN = PAIR + 2 * REACH_LAT
TILE = 16
HALF = TILE // 2
SPAN = 2 * TILE
LANES_K = 256
CLIP = 512.0
EPS = 1e-06
BF = jnp.bfloat16
F32 = jnp.float32
VMEM_LIMIT = 56 * 1024 * 1024
MIDDLE_LIMIT = 42 * 1024 * 1024
SMALL_LIMIT = 24 * 1024 * 1024


def band_picks(pairs):
    ext = PAIR * pairs + 2 * REACH_LAT
    pick = np.zeros((ext, ROW_TAPS, 2, pairs, PAIR, LANES_K // SPAN, SPAN))
    for p in range(pairs):
        for r in range(PAIR):
            for a in range(WIN):
                if 0 <= a - r < ROW_TAPS:
                    pick[PAIR * p + r + REACH_LAT, a - r, 0, p, r, a] = 1
                    pick[PAIR * p + a, r - a + 2 * REACH_LAT, 1, p, r, a] = 1
    return pick.reshape(ext * ROW_TAPS, 2, -1)


def band_kernel(pairs, which, values, index, reach, pick, out):
    lane = lax.broadcasted_iota(jnp.int32, (TILE, LANES_K), 1)
    j = lax.broadcasted_iota(jnp.int32, (TILE, LANES_K), 0)
    w = lane % SPAN
    ahead = jnp.where(w < HALF, w + TILE, w - TILE) - j
    tap = lax.broadcasted_iota(jnp.int32, values.shape, 0) - REACH_LON
    kept = jnp.where(jnp.abs(tap) <= reach[...], values[...], 0.0)
    for k in range(BASIS):
        taps = jnp.where(index[...] == k, kept, 0.0).astype(BF)
        spread = jnp.dot(taps, pick[...], preferred_element_type=F32)
        for p in range(pairs):
            for r in range(PAIR):
                first = (p * PAIR + r) * LANES_K
                block = jnp.zeros((TILE, LANES_K), F32)
                for b in range(COL_TAPS):
                    at = b - REACH_LON if which == 0 else REACH_LON - b
                    row = spread[b : b + 1, first : first + LANES_K]
                    block = jnp.where(ahead == at, row, block)
                at = (k * PAIR + r) * TILE
                out[p, at : at + TILE, :] = block[:, : WIN * SPAN].astype(BF)


def band_matrix(which, values, index, reach, pairs):
    return pl.pallas_call(
        functools.partial(band_kernel, pairs, which),
        out_shape=jax.ShapeDtypeStruct((pairs, BASIS * PAIR * TILE, WIN * SPAN), BF),
        compiler_params=params(SMALL_LIMIT),
        name="band_adjoint" if which else "band_forward",
    )(values, index, reach, jnp.asarray(band_picks(pairs)[:, which].reshape(values.shape[1], -1), BF))


def dot(a, b, ca, cb):
    return lax.dot_general(a, b, (((ca,), (cb,)), ((), ())), preferred_element_type=F32)


def window(rows, sides, m, tiles):
    parts = []
    for row, side in zip(rows, sides):
        if m + 1 < tiles:
            right = row[(m + 1) * TILE : (m + 2) * TILE, :].astype(F32)[:HALF]
        else:
            right = side[...].astype(F32)[:HALF]
        if m > 0:
            left = row[(m - 1) * TILE : m * TILE, :].astype(F32)[HALF:]
        else:
            left = side[...].astype(F32)[HALF:]
        parts.append(jnp.concatenate([right, left], axis=0).astype(BF))
        parts.append(row[m * TILE : (m + 1) * TILE, :])
    return jnp.concatenate(parts, axis=0)


def mixer_body(
    rows, sides, band, filt, w_in, w_out, cot, out, gf, edge, gin, gout, gfilt,
    y, low, hid, gact, act, gh,
):
    cols, chans = cot.shape[1:]
    tiles = cols // TILE
    cells = PAIR * cols
    for m in range(tiles):
        full = jnp.dot(band[0], window(rows, sides, m, tiles), preferred_element_type=F32)
        for r in range(PAIR):
            at = pl.ds(r * cols + m * TILE, TILE)
            total = None
            for k in range(BASIS):
                first = (k * PAIR + r) * TILE
                piece = full[first : first + TILE]
                y[k, at, :] = piece
                term = filt[k : k + 1, :] * piece
                total = term if total is None else total + term
            low[at, :] = total.astype(BF)
    cot_flat = cot[...].reshape(cells, chans)
    hid[...] = dot(low[...], w_in[...], 1, 0)
    gact[...] = dot(cot_flat, w_out[...], 1, 1)
    root = math.sqrt(2.0 / math.pi)
    for n in range(cells // TILE):
        at = pl.ds(n * TILE, TILE)
        v = hid[at, :]
        sq = v * v
        t = jnp.tanh(v * (root + (root * 0.044715) * sq))
        half = 0.5 + 0.5 * t
        act[at, :] = (v * half).astype(BF)
        slope = half + (0.5 * v) * (1.0 - t * t) * (root + (3 * root * 0.044715) * sq)
        gh[at, :] = (gact[at, :] * slope).astype(BF)
    back = dot(gh[...], w_in[...], 1, 1)
    mixed = dot(act[...], w_out[...], 1, 0)
    for r in range(PAIR):
        part = slice(r * cols, (r + 1) * cols)
        gf[r] = back[part].astype(BF)
        edge[r] = jnp.concatenate(
            [back[r * cols : r * cols + HALF], back[(r + 1) * cols - HALF : (r + 1) * cols]], axis=0
        ).astype(BF)
        out[r] = (rows[REACH_LAT + r][:cols, :].astype(F32) + mixed[part]).astype(BF)
    gout[...] += dot(cot_flat, act[...], 0, 0)
    gin[...] += dot(low[...], gh[...], 0, 0)
    lanes = 128
    for c in range(chans // lanes):
        at_c = pl.ds(c * lanes, lanes)
        sums = [gfilt[8 * k : 8 * k + 8, at_c] for k in range(BASIS)]
        for n in range(tiles):
            for r in range(PAIR):
                g = gf[r, pl.ds(n * TILE, TILE), at_c].astype(F32)
                for k in range(BASIS):
                    prod = g * y[k, pl.ds(r * cols + n * TILE, TILE), at_c]
                    sums[k] = sums[k] + (prod[:8] + prod[8:])
        for k in range(BASIS):
            gfilt[8 * k : 8 * k + 8, at_c] = sums[k]


def inner_kernel(x, side, band, filt, w_in, w_out, cot, out, gf, edge, gin, gout, gfilt, *scratch):
    i = pl.program_id(0)

    @pl.when(i == 0)
    def _():
        gin[...] = jnp.zeros_like(gin)
        gout[...] = jnp.zeros_like(gout)
        gfilt[...] = jnp.zeros_like(gfilt)

    rows = [x.at[PAIR * i + a] for a in range(WIN)]
    sides = [side.at[PAIR * i + a] for a in range(WIN)]
    mixer_body(rows, sides, band, filt, w_in, w_out, cot, out, gf, edge, gin, gout, gfilt, *scratch)


def place(win, at, part, side=None):
    n, cols = part.shape[:2]
    win[at : at + n, :cols, :] = part[...]
    if side is not None:
        win[at : at + n, cols:, :] = side[...]


def views(win):
    cols = win.shape[1] - TILE
    rows = [win.at[a] for a in range(WIN)]
    return rows, [win.at[a, pl.ds(cols, TILE)] for a in range(WIN)]


def beside_rows(gfilt, chans, per):
    bands, lanes = chans // per, 128
    mine = lax.broadcasted_iota(jnp.int32, (bands, chans), 1) // per == lax.broadcasted_iota(
        jnp.int32, (bands, chans), 0
    )
    lane = lax.broadcasted_iota(jnp.int32, (chans, lanes), 1)
    chan = lax.broadcasted_iota(jnp.int32, (chans, lanes), 0)
    packed = jnp.zeros((bands, lanes), F32)
    for k in range(BASIS):
        sums = jnp.sum(gfilt[8 * k : 8 * k + 8, :], axis=0, keepdims=True)
        spread = jnp.where(mine, sums, 0.0).astype(BF)
        fold = jnp.where((lane // per == k) & (lane % per == chan % per), 1.0, 0.0).astype(BF)
        packed = packed + jnp.dot(spread, fold, preferred_element_type=F32)
    row = lax.broadcasted_iota(jnp.int32, (chans, bands), 0) // per
    repeat = jnp.where(row == lax.broadcasted_iota(jnp.int32, (chans, bands), 1), 1.0, 0.0)
    return jnp.dot(repeat.astype(BF), packed.astype(BF), preferred_element_type=F32)


def outer_kernel(
    per, odd, x, side, lo, hi, band, filt, w_in, w_out, cot, partial_out, gin0, gout0, gfilt0,
    out, gf, edge, keep, give, win, gin, gout, gfilt, *scratch,
):
    i = pl.program_id(0)
    chans = gin.shape[0]

    @pl.when(i == 0)
    def _():
        gin[...] = gin0[...]
        gout[...] = gout0[...]
        gfilt[...] = gfilt0[...]
        place(win, 0, lo)
        place(win, REACH_LAT, x, side)

    @pl.when(i == 1)
    def _():
        place(win, 0, x, side)
        place(win, WIN - REACH_LAT, hi)

    rows, sides = views(win)
    mixer_body(rows, sides, band, filt, w_in, w_out, cot, out, gf, edge, gin, gout, gfilt, *scratch)

    @pl.when(i == 1)
    def _():
        beside = beside_rows(gfilt, chans, per)
        keep[:, chans:] = beside
        give[:, chans:] = beside.astype(BF)

    @pl.when((i == 1) & (odd[0] == 0))
    def _():
        keep[:, :chans] = gin[...]
        give[:, :chans] = gout[...].astype(BF)

    @pl.when((i == 1) & (odd[0] == 1))
    def _():
        keep[:, :chans] = gout[...]
        give[:, :chans] = gin[...].astype(BF)


def adjoint_body(rows, sides, band, filt, cot, out):
    cols = cot.shape[1]
    tiles = cols // TILE
    for m in range(tiles):
        full = jnp.dot(band[0], window(rows, sides, m, tiles), preferred_element_type=F32)
        at = slice(m * TILE, (m + 1) * TILE)
        for r in range(PAIR):
            total = cot[r, at, :].astype(F32)
            for k in range(BASIS):
                first = (k * PAIR + r) * TILE
                total = total + filt[k : k + 1, :] * full[first : first + TILE]
            out[r, at, :] = total.astype(BF)


def inner_adjoint(mid, mid_side, end, end_side, band, filt, cot, out, win):
    i = pl.program_id(0)

    @pl.when(i == 0)
    def _():
        place(win, 0, end, end_side)
        place(win, REACH_LAT, mid, mid_side)

    @pl.when(i == 1)
    def _():
        place(win, 0, mid, mid_side)
        place(win, WIN - REACH_LAT, end, end_side)

    adjoint_body(*views(win), band, filt, cot, out)


def outer_adjoint(mid, mid_side, end, end_side, lo, hi, band, filt, cot, partial_out, out, win):
    i = pl.program_id(0)
    place(win, REACH_LAT, end, end_side)

    @pl.when(i == 0)
    def _():
        place(win, 0, lo)
        place(win, WIN - REACH_LAT, mid, mid_side)

    @pl.when(i == 1)
    def _():
        place(win, 0, mid, mid_side)
        place(win, WIN - REACH_LAT, hi)

    adjoint_body(*views(win), band, filt, cot, out)


def blocks(n, shape, step=None):
    step = step or (lambda i: i)
    return pl.BlockSpec((n,) + shape[1:], lambda i: (step(i),) + (0,) * (len(shape) - 1))


def whole(shape):
    return pl.BlockSpec(shape, lambda i: (0,) * len(shape))


def params(limit=VMEM_LIMIT):
    return pltpu.CompilerParams(vmem_limit_bytes=limit)


def mixer_scratch(cols, chans):
    cells = PAIR * cols
    return [
        pltpu.VMEM((BASIS, cells, chans), F32),
        pltpu.VMEM((cells, chans), BF),
        pltpu.VMEM((cells, chans), F32),
        pltpu.VMEM((cells, chans), F32),
        pltpu.VMEM((cells, chans), BF),
        pltpu.VMEM((cells, chans), BF),
    ]


def mixer_cost(cols, chans):
    cells = 2 * PAIR * cols
    flops = 2 * cells * chans * (6 * chans + BASIS * WIN * SPAN)
    return pl.CostEstimate(
        flops=flops, bytes_accessed=10 * cells * chans, transcendentals=cells * chans
    )


def inner_pair(i):
    return 1 + i


def outer_pair(i):
    return 3 * i


def mixer_inner(x, side, band, filt, w_in, w_out, cot):
    rows, cols, chans = x.shape
    gf = jax.ShapeDtypeStruct((2 * PAIR, cols, chans), BF)
    edge = jax.ShapeDtypeStruct((2 * PAIR, TILE, chans), BF)
    matrix = jax.ShapeDtypeStruct((chans, chans), F32)
    small = jax.ShapeDtypeStruct((8 * BASIS, chans), F32)
    return pl.pallas_call(
        inner_kernel,
        grid=(2,),
        in_specs=[
            whole(x.shape), whole(side.shape), blocks(1, band.shape, inner_pair),
            whole(filt.shape), whole(w_in.shape), whole(w_out.shape),
            blocks(PAIR, cot.shape, inner_pair),
        ],
        out_specs=[
            blocks(PAIR, x.shape, inner_pair), blocks(PAIR, gf.shape), blocks(PAIR, edge.shape),
            whole(matrix.shape), whole(matrix.shape), whole(small.shape),
        ],
        out_shape=(jax.ShapeDtypeStruct(x.shape, BF), gf, edge, matrix, matrix, small),
        scratch_shapes=mixer_scratch(cols, chans),
        compiler_params=params(),
        cost_estimate=mixer_cost(cols, chans),
        name="mixer_inner",
    )(x, side, band, filt, w_in, w_out, cot)


def mixer_outer(
    odd, per, x, side, lo, hi, band, filt, w_in, w_out, cot, partial_out, sums
):
    rows, cols, chans = x.shape
    near = WIN - REACH_LAT
    gf = jax.ShapeDtypeStruct((2 * PAIR, cols, chans), BF)
    edge = jax.ShapeDtypeStruct((2 * PAIR, TILE, chans), BF)
    keep = jax.ShapeDtypeStruct((chans, chans + 128), F32)
    give = jax.ShapeDtypeStruct((chans, chans + 128), BF)
    return pl.pallas_call(
        functools.partial(outer_kernel, per),
        grid=(2,),
        in_specs=[
            pl.BlockSpec(memory_space=pltpu.SMEM),
            blocks(near, x.shape), blocks(near, side.shape),
            whole(lo.shape), whole(hi.shape),
            blocks(1, band.shape, outer_pair),
            whole(filt.shape), whole(w_in.shape), whole(w_out.shape),
            blocks(PAIR, cot.shape, outer_pair),
            pl.BlockSpec(memory_space=pl.ANY),
        ] + [whole(s.shape) for s in sums],
        out_specs=[
            blocks(PAIR, x.shape, outer_pair), blocks(PAIR, gf.shape), blocks(PAIR, edge.shape),
            whole(keep.shape), whole(give.shape),
        ],
        out_shape=(jax.ShapeDtypeStruct(x.shape, BF), gf, edge, keep, give),
        scratch_shapes=[
            pltpu.VMEM((WIN, cols + TILE, chans), BF),
            pltpu.VMEM((chans, chans), F32),
            pltpu.VMEM((chans, chans), F32),
            pltpu.VMEM((8 * BASIS, chans), F32),
        ] + mixer_scratch(cols, chans),
        input_output_aliases={10: 0},
        compiler_params=params(MIDDLE_LIMIT),
        cost_estimate=mixer_cost(cols, chans),
        name="mixer_outer",
    )(odd, x, side, lo, hi, band, filt, w_in, w_out, cot, partial_out, *sums)


def adjoint_cost(cols, chans):
    cells = 2 * PAIR * cols
    return pl.CostEstimate(
        flops=2 * cells * chans * BASIS * WIN * SPAN, bytes_accessed=6 * cells * chans,
        transcendentals=0,
    )


def adjoint_inner(mid, mid_side, end, end_side, band, filt, cot):
    rows, cols, chans = cot.shape
    return pl.pallas_call(
        inner_adjoint,
        grid=(2,),
        in_specs=[
            whole(mid.shape), whole(mid_side.shape),
            blocks(PAIR, end.shape), blocks(PAIR, end_side.shape),
            blocks(1, band.shape, inner_pair), whole(filt.shape),
            blocks(PAIR, cot.shape, inner_pair),
        ],
        out_specs=blocks(PAIR, cot.shape, inner_pair),
        out_shape=jax.ShapeDtypeStruct(cot.shape, BF),
        scratch_shapes=[pltpu.VMEM((WIN, cols + TILE, chans), BF)],
        compiler_params=params(SMALL_LIMIT),
        cost_estimate=adjoint_cost(cols, chans),
        name="adjoint_inner",
    )(mid, mid_side, end, end_side, band, filt, cot)


def adjoint_outer(mid, mid_side, end, end_side, lo, hi, band, filt, cot, partial_out):
    rows, cols, chans = cot.shape
    return pl.pallas_call(
        outer_adjoint,
        grid=(2,),
        in_specs=[
            blocks(PAIR, mid.shape), blocks(PAIR, mid_side.shape),
            blocks(PAIR, end.shape), blocks(PAIR, end_side.shape),
            whole(lo.shape), whole(hi.shape),
            blocks(1, band.shape, outer_pair), whole(filt.shape),
            blocks(PAIR, cot.shape, outer_pair),
            pl.BlockSpec(memory_space=pl.ANY),
        ],
        out_specs=blocks(PAIR, cot.shape, outer_pair),
        out_shape=jax.ShapeDtypeStruct(cot.shape, BF),
        scratch_shapes=[pltpu.VMEM((WIN, cols + TILE, chans), BF)],
        input_output_aliases={9: 0},
        compiler_params=params(),
        cost_estimate=adjoint_cost(cols, chans),
        name="adjoint_outer",
    )(mid, mid_side, end, end_side, lo, hi, band, filt, cot, partial_out)


def exchange_columns(first, last, count):
    up = [(i, (i + 1) % count) for i in range(count)]
    down = [(i, (i - 1) % count) for i in range(count)]
    right = lax.ppermute(first, "lon", down)
    left = lax.ppermute(last, "lon", up)
    return jnp.concatenate([right, left], axis=1)


def beside(rows, side):
    return jnp.concatenate([rows, side], axis=1)


def exchange_rows(first, last, count):
    up = [(i, i + 1) for i in range(count - 1)]
    down = [(i + 1, i) for i in range(count - 1)]
    return lax.ppermute(last, "lat", up), lax.ppermute(first, "lat", down)


def swap(a, count, bits):
    return lax.ppermute(a, "lon", [(i, i ^ bits) for i in range(count)])


def sum_kernel(chans, filters, copies, spread, share, square):
    total = jnp.sum(spread[...].astype(F32), axis=0)
    share[...] = total
    sq = total * total
    lane = lax.broadcasted_iota(jnp.int32, sq.shape, 1)
    row = lax.broadcasted_iota(jnp.int32, sq.shape, 0)
    beside = jnp.where((row == 0) & (lane < chans + filters), sq / copies, 0.0)
    square[...] = jnp.full(square.shape, jnp.sum(jnp.where(lane < chans, sq, beside)), F32)


def sum_shares(spread, chans, filters, copies):
    return pl.pallas_call(
        functools.partial(sum_kernel, chans, filters, copies),
        out_shape=(
            jax.ShapeDtypeStruct(spread.shape[1:], F32),
            jax.ShapeDtypeStruct((1, 128), F32),
        ),
        compiler_params=params(SMALL_LIMIT),
        name="sum_shares",
    )(spread)


def local(
    bands, panels,
    inputs, cotangent, basis_values, basis_index, lon_reach, filters, weight_in, weight_out,
):
    rows, cols, chans = inputs.shape
    pairs = rows // PAIR
    per = chans // bands
    first_row = lax.axis_index("lat") * rows
    ext = rows + 2 * REACH_LAT
    with jax.named_scope("input_halo"):
        side = exchange_columns(inputs[:, :HALF], inputs[:, cols - HALF :], panels)
        lo, hi = exchange_rows(
            beside(inputs[:REACH_LAT], side[:REACH_LAT]),
            beside(inputs[rows - REACH_LAT :], side[rows - REACH_LAT :]), bands,
        )
    with jax.named_scope("bands"):

        def cut(a):
            padded = jnp.pad(a, ((REACH_LAT, REACH_LAT),) + ((0, 0),) * (a.ndim - 1))
            return lax.dynamic_slice_in_dim(padded, first_row, ext, 0)

        tables = (
            cut(basis_values).reshape(-1, COL_TAPS).T,
            cut(basis_index).reshape(-1, COL_TAPS).T,
            cut(lon_reach).reshape(1, -1),
        )
        band = band_matrix(0, *tables, pairs)
        filt = filters.T
    out, gf_mid, edge_mid, *sums = mixer_inner(
        inputs, side, band, filt, weight_in, weight_out, cotangent
    )
    tables, out = lax.optimization_barrier((tables, out))
    band_adj = band_matrix(1, *tables, pairs)
    core = lax.axis_index("lon") % 2
    out, gf_end, edge_end, keep, give = mixer_outer(
        core.astype(jnp.int32).reshape(1), per, inputs, side, lo, hi, band, filt,
        weight_in, weight_out, cotangent, out, sums,
    )
    with jax.named_scope("grad_halo"):
        edge = jnp.concatenate([edge_end, edge_mid], axis=0)
        gside = exchange_columns(edge[:, :HALF], edge[:, HALF:], panels)
        end_side, mid_side = gside[: 2 * PAIR], gside[2 * PAIR :]
        ends = beside(gf_end[:PAIR], end_side[:PAIR]), beside(gf_end[PAIR:], end_side[PAIR:])
    back = adjoint_inner(gf_mid, mid_side, gf_end, end_side, band_adj, filt, cotangent)
    with jax.named_scope("reduce"):
        lanes, half = chans + 128, per // 2
        total = (keep + swap(give, panels, 1).astype(F32)).reshape(bands, per, lanes)
        upper = lax.axis_index("lon") // 2 == 1
        kept = jnp.where(upper, total[:, half:], total[:, :half])
        give = jnp.where(upper, total[:, :half], total[:, half:]).astype(BF)
        part = (kept + swap(give, panels, 2).astype(F32)).astype(BF)
        part, back, ends = lax.optimization_barrier((part, back, ends))
        halos = exchange_rows(*ends, bands)
        spread = lax.all_to_all(part, "lat", 0, 0)
    with jax.named_scope("norm"):
        share, square = sum_shares(spread, chans, BASIS * per, panels)
        mats, filt_row = share[:, :chans], share[:1, chans : chans + BASIS * per]
        near, across, far = (swap(mats, panels, bits) for bits in (2, 1, 3))
        every = lax.all_to_all(
            jnp.broadcast_to(square, (bands * panels, 1, 128)), ("lat", "lon"), 0, 0
        )
        near, across, far, every = lax.optimization_barrier((near, across, far, every))
        grad_total = jnp.sum(every[:, 0, 0])
        scale = jnp.minimum(jnp.float32(1.0), jnp.float32(CLIP) / jnp.sqrt(grad_total + EPS))

        def stack(own, other):
            return jnp.concatenate(
                [jnp.where(upper, other, own), jnp.where(upper, own, other)], axis=0
            )

        own, other = stack(mats, near), stack(across, far)
        odd = core == 1
        shares = (
            scale * jnp.where(odd, other, own),
            (scale * jnp.where(odd, own, other)).T,
            scale * filt_row.reshape(BASIS, per).T,
        )
    back = adjoint_outer(
        gf_mid, mid_side, gf_end, end_side, *halos, band_adj, filt, cotangent, back
    )
    return (out, back) + shares


def solution(mesh):
    bands, panels = mesh.shape["lat"], mesh.shape["lon"]
    field = P("lat", "lon", None)
    return jax.shard_map(
        functools.partial(local, bands, panels),
        mesh=mesh,
        in_specs=(field, field, P(), P(), P(), P(), P(), P()),
        out_specs=(field, field, P("lat", None), P(None, "lat"), P("lat", None)),
        check_vma=False,
    )
```

```python
import functools
import math

import jax
import jax.numpy as jnp
import numpy as np
from jax import lax
from jax.experimental import pallas as pl
from jax.experimental.pallas import tpu as pltpu
from jax.sharding import PartitionSpec as P

BASIS = 9
REACH_LAT = 2
REACH_LON = 4
ROW_TAPS = 2 * REACH_LAT + 1
COL_TAPS = 2 * REACH_LON + 1
PAIR = 2
WIN = PAIR + 2 * REACH_LAT
TILE = 16
HALF = TILE // 2
SPAN = 2 * TILE
LANES_K = 256
CLIP = 512.0
EPS = 1e-06
BF = jnp.bfloat16
F32 = jnp.float32
VMEM_LIMIT = 56 * 1024 * 1024
SMALL_LIMIT = 24 * 1024 * 1024


def band_picks(pairs):
    ext = PAIR * pairs + 2 * REACH_LAT
    pick = np.zeros((ext, ROW_TAPS, 2, pairs, PAIR, LANES_K // SPAN, SPAN))
    for p in range(pairs):
        for r in range(PAIR):
            for a in range(WIN):
                if 0 <= a - r < ROW_TAPS:
                    pick[PAIR * p + r + REACH_LAT, a - r, 0, p, r, a] = 1
                    pick[PAIR * p + a, r - a + 2 * REACH_LAT, 1, p, r, a] = 1
    return pick.reshape(ext * ROW_TAPS, 2, -1)


def band_kernel(pairs, which, values, index, reach, pick, out):
    lane = lax.broadcasted_iota(jnp.int32, (TILE, LANES_K), 1)
    j = lax.broadcasted_iota(jnp.int32, (TILE, LANES_K), 0)
    w = lane % SPAN
    ahead = jnp.where(w < HALF, w + TILE, w - TILE) - j
    tap = lax.broadcasted_iota(jnp.int32, values.shape, 0) - REACH_LON
    kept = jnp.where(jnp.abs(tap) <= reach[...], values[...], 0.0)
    for k in range(BASIS):
        taps = jnp.where(index[...] == k, kept, 0.0).astype(BF)
        spread = jnp.dot(taps, pick[...], preferred_element_type=F32)
        for p in range(pairs):
            for r in range(PAIR):
                first = (p * PAIR + r) * LANES_K
                block = jnp.zeros((TILE, LANES_K), F32)
                for b in range(COL_TAPS):
                    at = b - REACH_LON if which == 0 else REACH_LON - b
                    row = spread[b : b + 1, first : first + LANES_K]
                    block = jnp.where(ahead == at, row, block)
                at = (k * PAIR + r) * TILE
                out[p, at : at + TILE, :] = block[:, : WIN * SPAN].astype(BF)


def band_matrix(which, values, index, reach, pairs):
    return pl.pallas_call(
        functools.partial(band_kernel, pairs, which),
        out_shape=jax.ShapeDtypeStruct((pairs, BASIS * PAIR * TILE, WIN * SPAN), BF),
        compiler_params=params(SMALL_LIMIT),
        name="band_adjoint" if which else "band_forward",
    )(values, index, reach, jnp.asarray(band_picks(pairs)[:, which].reshape(values.shape[1], -1), BF))


def dot(a, b, ca, cb):
    return lax.dot_general(a, b, (((ca,), (cb,)), ((), ())), preferred_element_type=F32)


def window(rows, sides, m, tiles):
    parts = []
    for row, side in zip(rows, sides):
        if m + 1 < tiles:
            right = row[(m + 1) * TILE : (m + 2) * TILE, :].astype(F32)[:HALF]
        else:
            right = side[...].astype(F32)[:HALF]
        if m > 0:
            left = row[(m - 1) * TILE : m * TILE, :].astype(F32)[HALF:]
        else:
            left = side[...].astype(F32)[HALF:]
        parts.append(jnp.concatenate([right, left], axis=0).astype(BF))
        parts.append(row[m * TILE : (m + 1) * TILE, :])
    return jnp.concatenate(parts, axis=0)


def mixer_body(
    rows, sides, band, filt, w_in, w_out, cot, out, gf, edge, gin, gout, gfilt,
    y, low, hid, gact, act, gh,
):
    cols, chans = cot.shape[1:]
    tiles = cols // TILE
    cells = PAIR * cols
    for m in range(tiles):
        full = jnp.dot(band[0], window(rows, sides, m, tiles), preferred_element_type=F32)
        for r in range(PAIR):
            at = pl.ds(r * cols + m * TILE, TILE)
            total = None
            for k in range(BASIS):
                first = (k * PAIR + r) * TILE
                piece = full[first : first + TILE]
                y[k, at, :] = piece
                term = filt[k : k + 1, :] * piece
                total = term if total is None else total + term
            low[at, :] = total.astype(BF)
    cot_flat = cot[...].reshape(cells, chans)
    hid[...] = dot(low[...], w_in[...], 1, 0)
    gact[...] = dot(cot_flat, w_out[...], 1, 1)
    root = math.sqrt(2.0 / math.pi)
    for n in range(cells // TILE):
        at = pl.ds(n * TILE, TILE)
        v = hid[at, :]
        sq = v * v
        t = jnp.tanh(v * (root + (root * 0.044715) * sq))
        half = 0.5 + 0.5 * t
        act[at, :] = (v * half).astype(BF)
        slope = half + (0.5 * v) * (1.0 - t * t) * (root + (3 * root * 0.044715) * sq)
        gh[at, :] = (gact[at, :] * slope).astype(BF)
    back = dot(gh[...], w_in[...], 1, 1)
    mixed = dot(act[...], w_out[...], 1, 0)
    for r in range(PAIR):
        part = slice(r * cols, (r + 1) * cols)
        gf[r] = back[part].astype(BF)
        edge[r] = jnp.concatenate(
            [back[r * cols : r * cols + HALF], back[(r + 1) * cols - HALF : (r + 1) * cols]], axis=0
        ).astype(BF)
        out[r] = (rows[REACH_LAT + r][:cols, :].astype(F32) + mixed[part]).astype(BF)
    gout[...] += dot(cot_flat, act[...], 0, 0)
    gin[...] += dot(low[...], gh[...], 0, 0)
    lanes = 128
    for c in range(chans // lanes):
        at_c = pl.ds(c * lanes, lanes)
        sums = [gfilt[8 * k : 8 * k + 8, at_c] for k in range(BASIS)]
        for n in range(tiles):
            for r in range(PAIR):
                g = gf[r, pl.ds(n * TILE, TILE), at_c].astype(F32)
                for k in range(BASIS):
                    prod = g * y[k, pl.ds(r * cols + n * TILE, TILE), at_c]
                    sums[k] = sums[k] + (prod[:8] + prod[8:])
        for k in range(BASIS):
            gfilt[8 * k : 8 * k + 8, at_c] = sums[k]


def inner_kernel(x, side, band, filt, w_in, w_out, cot, out, gf, edge, gin, gout, gfilt, *scratch):
    i = pl.program_id(0)

    @pl.when(i == 0)
    def _():
        gin[...] = jnp.zeros_like(gin)
        gout[...] = jnp.zeros_like(gout)
        gfilt[...] = jnp.zeros_like(gfilt)

    rows = [x.at[PAIR * i + a] for a in range(WIN)]
    sides = [side.at[PAIR * i + a] for a in range(WIN)]
    mixer_body(rows, sides, band, filt, w_in, w_out, cot, out, gf, edge, gin, gout, gfilt, *scratch)


def place(win, at, part, side=None):
    n, cols = part.shape[:2]
    win[at : at + n, :cols, :] = part[...]
    if side is not None:
        win[at : at + n, cols:, :] = side[...]


def views(win):
    cols = win.shape[1] - TILE
    rows = [win.at[a] for a in range(WIN)]
    return rows, [win.at[a, pl.ds(cols, TILE)] for a in range(WIN)]


def beside_rows(gfilt, chans, per):
    bands, lanes = chans // per, 128
    mine = lax.broadcasted_iota(jnp.int32, (bands, chans), 1) // per == lax.broadcasted_iota(
        jnp.int32, (bands, chans), 0
    )
    lane = lax.broadcasted_iota(jnp.int32, (chans, lanes), 1)
    chan = lax.broadcasted_iota(jnp.int32, (chans, lanes), 0)
    packed = jnp.zeros((bands, lanes), F32)
    for k in range(BASIS):
        sums = jnp.sum(gfilt[8 * k : 8 * k + 8, :], axis=0, keepdims=True)
        spread = jnp.where(mine, sums, 0.0).astype(BF)
        fold = jnp.where((lane // per == k) & (lane % per == chan % per), 1.0, 0.0).astype(BF)
        packed = packed + jnp.dot(spread, fold, preferred_element_type=F32)
    row = lax.broadcasted_iota(jnp.int32, (chans, bands), 0) // per
    repeat = jnp.where(row == lax.broadcasted_iota(jnp.int32, (chans, bands), 1), 1.0, 0.0)
    return jnp.dot(repeat.astype(BF), packed.astype(BF), preferred_element_type=F32)


def outer_kernel(
    per, odd, x, side, lo, hi, band, filt, w_in, w_out, cot, partial_out, gin0, gout0, gfilt0,
    out, gf, edge, keep, give, win, gin, gout, gfilt, *scratch,
):
    i = pl.program_id(0)
    chans = gin.shape[0]

    @pl.when(i == 0)
    def _():
        gin[...] = gin0[...]
        gout[...] = gout0[...]
        gfilt[...] = gfilt0[...]
        place(win, 0, lo)
        place(win, REACH_LAT, x, side)

    @pl.when(i == 1)
    def _():
        place(win, 0, x, side)
        place(win, WIN - REACH_LAT, hi)

    rows, sides = views(win)
    mixer_body(rows, sides, band, filt, w_in, w_out, cot, out, gf, edge, gin, gout, gfilt, *scratch)

    @pl.when(i == 1)
    def _():
        beside = beside_rows(gfilt, chans, per)
        keep[:, chans:] = beside
        give[:, chans:] = beside.astype(BF)

    @pl.when((i == 1) & (odd[0] == 0))
    def _():
        keep[:, :chans] = gin[...]
        give[:, :chans] = gout[...].astype(BF)

    @pl.when((i == 1) & (odd[0] == 1))
    def _():
        keep[:, :chans] = gout[...]
        give[:, :chans] = gin[...].astype(BF)


def adjoint_body(rows, sides, band, filt, cot, out):
    cols = cot.shape[1]
    tiles = cols // TILE
    for m in range(tiles):
        full = jnp.dot(band[0], window(rows, sides, m, tiles), preferred_element_type=F32)
        at = slice(m * TILE, (m + 1) * TILE)
        for r in range(PAIR):
            total = cot[r, at, :].astype(F32)
            for k in range(BASIS):
                first = (k * PAIR + r) * TILE
                total = total + filt[k : k + 1, :] * full[first : first + TILE]
            out[r, at, :] = total.astype(BF)


def inner_adjoint(mid, mid_side, end, end_side, band, filt, cot, out, win):
    i = pl.program_id(0)

    @pl.when(i == 0)
    def _():
        place(win, 0, end, end_side)
        place(win, REACH_LAT, mid, mid_side)

    @pl.when(i == 1)
    def _():
        place(win, 0, mid, mid_side)
        place(win, WIN - REACH_LAT, end, end_side)

    adjoint_body(*views(win), band, filt, cot, out)


def outer_adjoint(mid, mid_side, end, end_side, lo, hi, band, filt, cot, partial_out, out, win):
    i = pl.program_id(0)
    place(win, REACH_LAT, end, end_side)

    @pl.when(i == 0)
    def _():
        place(win, 0, lo)
        place(win, WIN - REACH_LAT, mid, mid_side)

    @pl.when(i == 1)
    def _():
        place(win, 0, mid, mid_side)
        place(win, WIN - REACH_LAT, hi)

    adjoint_body(*views(win), band, filt, cot, out)


def blocks(n, shape, step=None):
    step = step or (lambda i: i)
    return pl.BlockSpec((n,) + shape[1:], lambda i: (step(i),) + (0,) * (len(shape) - 1))


def whole(shape):
    return pl.BlockSpec(shape, lambda i: (0,) * len(shape))


def params(limit=VMEM_LIMIT):
    return pltpu.CompilerParams(vmem_limit_bytes=limit)


def mixer_scratch(cols, chans):
    cells = PAIR * cols
    return [
        pltpu.VMEM((BASIS, cells, chans), F32),
        pltpu.VMEM((cells, chans), BF),
        pltpu.VMEM((cells, chans), F32),
        pltpu.VMEM((cells, chans), F32),
        pltpu.VMEM((cells, chans), BF),
        pltpu.VMEM((cells, chans), BF),
    ]


def mixer_cost(cols, chans):
    cells = 2 * PAIR * cols
    flops = 2 * cells * chans * (6 * chans + BASIS * WIN * SPAN)
    return pl.CostEstimate(
        flops=flops, bytes_accessed=10 * cells * chans, transcendentals=cells * chans
    )


def inner_pair(i):
    return 1 + i


def outer_pair(i):
    return 3 * i


def mixer_inner(x, side, band, filt, w_in, w_out, cot):
    rows, cols, chans = x.shape
    gf = jax.ShapeDtypeStruct((2 * PAIR, cols, chans), BF)
    edge = jax.ShapeDtypeStruct((2 * PAIR, TILE, chans), BF)
    matrix = jax.ShapeDtypeStruct((chans, chans), F32)
    small = jax.ShapeDtypeStruct((8 * BASIS, chans), F32)
    return pl.pallas_call(
        inner_kernel,
        grid=(2,),
        in_specs=[
            whole(x.shape), whole(side.shape), blocks(1, band.shape, inner_pair),
            whole(filt.shape), whole(w_in.shape), whole(w_out.shape),
            blocks(PAIR, cot.shape, inner_pair),
        ],
        out_specs=[
            blocks(PAIR, x.shape, inner_pair), blocks(PAIR, gf.shape), blocks(PAIR, edge.shape),
            whole(matrix.shape), whole(matrix.shape), whole(small.shape),
        ],
        out_shape=(jax.ShapeDtypeStruct(x.shape, BF), gf, edge, matrix, matrix, small),
        scratch_shapes=mixer_scratch(cols, chans),
        compiler_params=params(),
        cost_estimate=mixer_cost(cols, chans),
        name="mixer_inner",
    )(x, side, band, filt, w_in, w_out, cot)


def mixer_outer(
    odd, per, x, side, lo, hi, band, filt, w_in, w_out, cot, partial_out, sums
):
    rows, cols, chans = x.shape
    near = WIN - REACH_LAT
    gf = jax.ShapeDtypeStruct((2 * PAIR, cols, chans), BF)
    edge = jax.ShapeDtypeStruct((2 * PAIR, TILE, chans), BF)
    keep = jax.ShapeDtypeStruct((chans, chans + 128), F32)
    give = jax.ShapeDtypeStruct((chans, chans + 128), BF)
    return pl.pallas_call(
        functools.partial(outer_kernel, per),
        grid=(2,),
        in_specs=[
            pl.BlockSpec(memory_space=pltpu.SMEM),
            blocks(near, x.shape), blocks(near, side.shape),
            whole(lo.shape), whole(hi.shape),
            blocks(1, band.shape, outer_pair),
            whole(filt.shape), whole(w_in.shape), whole(w_out.shape),
            blocks(PAIR, cot.shape, outer_pair),
            pl.BlockSpec(memory_space=pl.ANY),
        ] + [whole(s.shape) for s in sums],
        out_specs=[
            blocks(PAIR, x.shape, outer_pair), blocks(PAIR, gf.shape), blocks(PAIR, edge.shape),
            whole(keep.shape), whole(give.shape),
        ],
        out_shape=(jax.ShapeDtypeStruct(x.shape, BF), gf, edge, keep, give),
        scratch_shapes=[
            pltpu.VMEM((WIN, cols + TILE, chans), BF),
            pltpu.VMEM((chans, chans), F32),
            pltpu.VMEM((chans, chans), F32),
            pltpu.VMEM((8 * BASIS, chans), F32),
        ] + mixer_scratch(cols, chans),
        input_output_aliases={10: 0},
        compiler_params=params(),
        cost_estimate=mixer_cost(cols, chans),
        name="mixer_outer",
    )(odd, x, side, lo, hi, band, filt, w_in, w_out, cot, partial_out, *sums)


def adjoint_cost(cols, chans):
    cells = 2 * PAIR * cols
    return pl.CostEstimate(
        flops=2 * cells * chans * BASIS * WIN * SPAN, bytes_accessed=6 * cells * chans,
        transcendentals=0,
    )


def adjoint_inner(mid, mid_side, end, end_side, band, filt, cot):
    rows, cols, chans = cot.shape
    return pl.pallas_call(
        inner_adjoint,
        grid=(2,),
        in_specs=[
            whole(mid.shape), whole(mid_side.shape),
            blocks(PAIR, end.shape), blocks(PAIR, end_side.shape),
            blocks(1, band.shape, inner_pair), whole(filt.shape),
            blocks(PAIR, cot.shape, inner_pair),
        ],
        out_specs=blocks(PAIR, cot.shape, inner_pair),
        out_shape=jax.ShapeDtypeStruct(cot.shape, BF),
        scratch_shapes=[pltpu.VMEM((WIN, cols + TILE, chans), BF)],
        compiler_params=params(SMALL_LIMIT),
        cost_estimate=adjoint_cost(cols, chans),
        name="adjoint_inner",
    )(mid, mid_side, end, end_side, band, filt, cot)


def adjoint_outer(mid, mid_side, end, end_side, lo, hi, band, filt, cot, partial_out):
    rows, cols, chans = cot.shape
    return pl.pallas_call(
        outer_adjoint,
        grid=(2,),
        in_specs=[
            blocks(PAIR, mid.shape), blocks(PAIR, mid_side.shape),
            blocks(PAIR, end.shape), blocks(PAIR, end_side.shape),
            whole(lo.shape), whole(hi.shape),
            blocks(1, band.shape, outer_pair), whole(filt.shape),
            blocks(PAIR, cot.shape, outer_pair),
            pl.BlockSpec(memory_space=pl.ANY),
        ],
        out_specs=blocks(PAIR, cot.shape, outer_pair),
        out_shape=jax.ShapeDtypeStruct(cot.shape, BF),
        scratch_shapes=[pltpu.VMEM((WIN, cols + TILE, chans), BF)],
        input_output_aliases={9: 0},
        compiler_params=params(),
        cost_estimate=adjoint_cost(cols, chans),
        name="adjoint_outer",
    )(mid, mid_side, end, end_side, lo, hi, band, filt, cot, partial_out)


def exchange_columns(first, last, count):
    up = [(i, (i + 1) % count) for i in range(count)]
    down = [(i, (i - 1) % count) for i in range(count)]
    right = lax.ppermute(first, "lon", down)
    left = lax.ppermute(last, "lon", up)
    return jnp.concatenate([right, left], axis=1)


def beside(rows, side):
    return jnp.concatenate([rows, side], axis=1)


def exchange_rows(first, last, count):
    up = [(i, i + 1) for i in range(count - 1)]
    down = [(i + 1, i) for i in range(count - 1)]
    return lax.ppermute(last, "lat", up), lax.ppermute(first, "lat", down)


def swap(a, count, bits):
    return lax.ppermute(a, "lon", [(i, i ^ bits) for i in range(count)])


def sum_kernel(chans, filters, copies, spread, share, square):
    total = jnp.sum(spread[...].astype(F32), axis=0)
    share[...] = total
    sq = total * total
    lane = lax.broadcasted_iota(jnp.int32, sq.shape, 1)
    row = lax.broadcasted_iota(jnp.int32, sq.shape, 0)
    beside = jnp.where((row == 0) & (lane < chans + filters), sq / copies, 0.0)
    square[...] = jnp.full(square.shape, jnp.sum(jnp.where(lane < chans, sq, beside)), F32)


def sum_shares(spread, chans, filters, copies):
    return pl.pallas_call(
        functools.partial(sum_kernel, chans, filters, copies),
        out_shape=(
            jax.ShapeDtypeStruct(spread.shape[1:], F32),
            jax.ShapeDtypeStruct((1, 128), F32),
        ),
        compiler_params=params(SMALL_LIMIT),
        name="sum_shares",
    )(spread)


def scale_kernel(per, flags, every, mats, near, across, far, beside, w_in, w_out, filters, work):
    total = jnp.sum(every[...], axis=0)
    scale = jnp.minimum(1.0, CLIP / jnp.sqrt(total + EPS))[:, :1]
    half = mats.shape[0]
    upper = jnp.full(mats.shape, flags[1], jnp.int32) == 1
    for n, (own, other) in enumerate(((mats, near), (across, far))):
        work[n, :half, :] = jnp.where(upper, other[...], own[...]) * scale
        work[n, half:, :] = jnp.where(upper, own[...], other[...]) * scale
    odd = jnp.full(w_in.shape, flags[0], jnp.int32) == 1
    w_in[...] = jnp.where(odd, work[1], work[0])
    w_out[...] = jnp.where(odd, work[0], work[1]).T
    lanes = beside.shape[1]
    lane = lax.broadcasted_iota(jnp.int32, (per, lanes), 1)
    chan = lax.broadcasted_iota(jnp.int32, (per, lanes), 0)
    spread = jnp.where(lane % per == chan, beside[...], 0.0)
    at = lax.broadcasted_iota(jnp.int32, (lanes, BASIS), 0) // per
    fold = jnp.where(at == lax.broadcasted_iota(jnp.int32, (lanes, BASIS), 1), 1.0, 0.0)
    sums = jnp.dot(spread, fold, precision=lax.Precision.HIGHEST, preferred_element_type=F32)
    filters[...] = sums * scale


def scaled(flags, every, mats, near, across, far, beside, per):
    chans = mats.shape[1]
    blocks_in = [pl.BlockSpec(memory_space=pltpu.SMEM)]
    blocks_in += [pl.BlockSpec(memory_space=pltpu.VMEM)] * 6
    return pl.pallas_call(
        functools.partial(scale_kernel, per),
        in_specs=blocks_in,
        out_shape=(
            jax.ShapeDtypeStruct((per, chans), F32),
            jax.ShapeDtypeStruct((chans, per), F32),
            jax.ShapeDtypeStruct((per, BASIS), F32),
        ),
        scratch_shapes=[pltpu.VMEM((2, per, chans), F32)],
        compiler_params=params(SMALL_LIMIT),
        name="scaled",
    )(flags, every, mats, near, across, far, beside)


def local(
    bands, panels,
    inputs, cotangent, basis_values, basis_index, lon_reach, filters, weight_in, weight_out,
):
    rows, cols, chans = inputs.shape
    pairs = rows // PAIR
    per = chans // bands
    first_row = lax.axis_index("lat") * rows
    ext = rows + 2 * REACH_LAT
    with jax.named_scope("input_halo"):
        side = exchange_columns(inputs[:, :HALF], inputs[:, cols - HALF :], panels)
        lo, hi = exchange_rows(
            beside(inputs[:REACH_LAT], side[:REACH_LAT]),
            beside(inputs[rows - REACH_LAT :], side[rows - REACH_LAT :]), bands,
        )
    with jax.named_scope("bands"):

        def cut(a):
            padded = jnp.pad(a, ((REACH_LAT, REACH_LAT),) + ((0, 0),) * (a.ndim - 1))
            return lax.dynamic_slice_in_dim(padded, first_row, ext, 0)

        tables = (
            cut(basis_values).reshape(-1, COL_TAPS).T,
            cut(basis_index).reshape(-1, COL_TAPS).T,
            cut(lon_reach).reshape(1, -1),
        )
        band = band_matrix(0, *tables, pairs)
        filt = filters.T
    out, gf_mid, edge_mid, *sums = mixer_inner(
        inputs, side, band, filt, weight_in, weight_out, cotangent
    )
    tables, out = lax.optimization_barrier((tables, out))
    band_adj = band_matrix(1, *tables, pairs)
    core = lax.axis_index("lon") % 2
    out, gf_end, edge_end, keep, give = mixer_outer(
        core.astype(jnp.int32).reshape(1), per, inputs, side, lo, hi, band, filt,
        weight_in, weight_out, cotangent, out, sums,
    )
    with jax.named_scope("grad_halo"):
        edge = jnp.concatenate([edge_end, edge_mid], axis=0)
        gside = exchange_columns(edge[:, :HALF], edge[:, HALF:], panels)
        end_side, mid_side = gside[: 2 * PAIR], gside[2 * PAIR :]
        ends = beside(gf_end[:PAIR], end_side[:PAIR]), beside(gf_end[PAIR:], end_side[PAIR:])
    back = adjoint_inner(gf_mid, mid_side, gf_end, end_side, band_adj, filt, cotangent)
    with jax.named_scope("reduce"):
        lanes, half = chans + 128, per // 2
        total = (keep + swap(give, panels, 1).astype(F32)).reshape(bands, per, lanes)
        upper = lax.axis_index("lon") // 2 == 1
        kept = jnp.where(upper, total[:, half:], total[:, :half])
        give = jnp.where(upper, total[:, :half], total[:, half:]).astype(BF)
        part = (kept + swap(give, panels, 2).astype(F32)).astype(BF)
        part, back, ends = lax.optimization_barrier((part, back, ends))
        halos = exchange_rows(*ends, bands)
        spread = lax.all_to_all(part, "lat", 0, 0)
    with jax.named_scope("norm"):
        share, square = sum_shares(spread, chans, BASIS * per, panels)
        mats = share[:, :chans]
        near, across, far = (swap(mats, panels, bits) for bits in (2, 1, 3))
        every = lax.all_to_all(
            jnp.broadcast_to(square, (bands * panels, 1, 128)), ("lat", "lon"), 0, 0
        )
        near, across, far, every = lax.optimization_barrier((near, across, far, every))
        flags = jnp.stack([core, lax.axis_index("lon") // 2]).astype(jnp.int32)
        shares = scaled(flags, every, mats, near, across, far, share[:1, chans:], per)
    back = adjoint_outer(
        gf_mid, mid_side, gf_end, end_side, *halos, band_adj, filt, cotangent, back
    )
    return (out, back, *shares)


def solution(mesh):
    bands, panels = mesh.shape["lat"], mesh.shape["lon"]
    field = P("lat", "lon", None)
    return jax.shard_map(
        functools.partial(local, bands, panels),
        mesh=mesh,
        in_specs=(field, field, P(), P(), P(), P(), P(), P()),
        out_specs=(field, field, P("lat", None), P(None, "lat"), P("lat", None)),
        check_vma=False,
    )
```

```python
import functools
import math

import jax
import jax.numpy as jnp
import numpy as np
from jax import lax
from jax.experimental import pallas as pl
from jax.experimental.pallas import tpu as pltpu
from jax.sharding import PartitionSpec as P

BASIS = 9
REACH_LAT = 2
REACH_LON = 4
ROW_TAPS = 2 * REACH_LAT + 1
COL_TAPS = 2 * REACH_LON + 1
PAIR = 2
WIN = PAIR + 2 * REACH_LAT
TILE = 16
HALF = TILE // 2
SPAN = 2 * TILE
LANES_K = 256
CLIP = 512.0
EPS = 1e-06
BF = jnp.bfloat16
F32 = jnp.float32
VMEM_LIMIT = 56 * 1024 * 1024
SMALL_LIMIT = 24 * 1024 * 1024


def band_picks(pairs):
    ext = PAIR * pairs + 2 * REACH_LAT
    pick = np.zeros((ext, ROW_TAPS, 2, pairs, PAIR, LANES_K // SPAN, SPAN))
    for p in range(pairs):
        for r in range(PAIR):
            for a in range(WIN):
                if 0 <= a - r < ROW_TAPS:
                    pick[PAIR * p + r + REACH_LAT, a - r, 0, p, r, a] = 1
                    pick[PAIR * p + a, r - a + 2 * REACH_LAT, 1, p, r, a] = 1
    return pick.reshape(ext * ROW_TAPS, 2, -1)


def band_kernel(pairs, which, values, index, reach, pick, out):
    lane = lax.broadcasted_iota(jnp.int32, (TILE, LANES_K), 1)
    j = lax.broadcasted_iota(jnp.int32, (TILE, LANES_K), 0)
    w = lane % SPAN
    ahead = jnp.where(w < HALF, w + TILE, w - TILE) - j
    tap = lax.broadcasted_iota(jnp.int32, values.shape, 0) - REACH_LON
    kept = jnp.where(jnp.abs(tap) <= reach[...], values[...], 0.0)
    for k in range(BASIS):
        taps = jnp.where(index[...] == k, kept, 0.0).astype(BF)
        spread = jnp.dot(taps, pick[...], preferred_element_type=F32)
        for p in range(pairs):
            for r in range(PAIR):
                first = (p * PAIR + r) * LANES_K
                block = jnp.zeros((TILE, LANES_K), F32)
                for b in range(COL_TAPS):
                    at = b - REACH_LON if which == 0 else REACH_LON - b
                    row = spread[b : b + 1, first : first + LANES_K]
                    block = jnp.where(ahead == at, row, block)
                at = (k * PAIR + r) * TILE
                out[p, at : at + TILE, :] = block[:, : WIN * SPAN].astype(BF)


def band_matrix(which, values, index, reach, pairs):
    return pl.pallas_call(
        functools.partial(band_kernel, pairs, which),
        out_shape=jax.ShapeDtypeStruct((pairs, BASIS * PAIR * TILE, WIN * SPAN), BF),
        compiler_params=params(SMALL_LIMIT),
        name="band_adjoint" if which else "band_forward",
    )(values, index, reach, jnp.asarray(band_picks(pairs)[:, which].reshape(values.shape[1], -1), BF))


def dot(a, b, ca, cb):
    return lax.dot_general(a, b, (((ca,), (cb,)), ((), ())), preferred_element_type=F32)


def window(rows, sides, m, tiles):
    parts = []
    for row, side in zip(rows, sides):
        if m + 1 < tiles:
            right = row[(m + 1) * TILE : (m + 2) * TILE, :].astype(F32)[:HALF]
        else:
            right = side[...].astype(F32)[:HALF]
        if m > 0:
            left = row[(m - 1) * TILE : m * TILE, :].astype(F32)[HALF:]
        else:
            left = side[...].astype(F32)[HALF:]
        parts.append(jnp.concatenate([right, left], axis=0).astype(BF))
        parts.append(row[m * TILE : (m + 1) * TILE, :])
    return jnp.concatenate(parts, axis=0)


def mixer_body(
    rows, sides, band, filt, w_in, w_out, cot, out, gf, edge, gin, gout, gfilt,
    y, low, hid, gact, act, gh,
):
    cols, chans = cot.shape[1:]
    tiles = cols // TILE
    cells = PAIR * cols
    for m in range(tiles):
        full = jnp.dot(band[0], window(rows, sides, m, tiles), preferred_element_type=F32)
        for r in range(PAIR):
            at = pl.ds(r * cols + m * TILE, TILE)
            total = None
            for k in range(BASIS):
                first = (k * PAIR + r) * TILE
                piece = full[first : first + TILE]
                y[k, at, :] = piece
                term = filt[k : k + 1, :] * piece
                total = term if total is None else total + term
            low[at, :] = total.astype(BF)
    cot_flat = cot[...].reshape(cells, chans)
    hid[...] = dot(low[...], w_in[...], 1, 0)
    gact[...] = dot(cot_flat, w_out[...], 1, 1)
    root = math.sqrt(2.0 / math.pi)
    for n in range(cells // TILE):
        at = pl.ds(n * TILE, TILE)
        v = hid[at, :]
        sq = v * v
        t = jnp.tanh(v * (root + (root * 0.044715) * sq))
        half = 0.5 + 0.5 * t
        act[at, :] = (v * half).astype(BF)
        slope = half + (0.5 * v) * (1.0 - t * t) * (root + (3 * root * 0.044715) * sq)
        gh[at, :] = (gact[at, :] * slope).astype(BF)
    back = dot(gh[...], w_in[...], 1, 1)
    mixed = dot(act[...], w_out[...], 1, 0)
    for r in range(PAIR):
        part = slice(r * cols, (r + 1) * cols)
        gf[r] = back[part].astype(BF)
        edge[r] = jnp.concatenate(
            [back[r * cols : r * cols + HALF], back[(r + 1) * cols - HALF : (r + 1) * cols]], axis=0
        ).astype(BF)
        out[r] = (rows[REACH_LAT + r][:cols, :].astype(F32) + mixed[part]).astype(BF)
    gout[...] += dot(cot_flat, act[...], 0, 0)
    gin[...] += dot(low[...], gh[...], 0, 0)
    lanes = 128
    for c in range(chans // lanes):
        at_c = pl.ds(c * lanes, lanes)
        sums = [gfilt[8 * k : 8 * k + 8, at_c] for k in range(BASIS)]
        for n in range(tiles):
            for r in range(PAIR):
                g = gf[r, pl.ds(n * TILE, TILE), at_c].astype(F32)
                for k in range(BASIS):
                    prod = g * y[k, pl.ds(r * cols + n * TILE, TILE), at_c]
                    sums[k] = sums[k] + (prod[:8] + prod[8:])
        for k in range(BASIS):
            gfilt[8 * k : 8 * k + 8, at_c] = sums[k]


def inner_kernel(x, side, band, filt, w_in, w_out, cot, out, gf, edge, gin, gout, gfilt, *scratch):
    i = pl.program_id(0)

    @pl.when(i == 0)
    def _():
        gin[...] = jnp.zeros_like(gin)
        gout[...] = jnp.zeros_like(gout)
        gfilt[...] = jnp.zeros_like(gfilt)

    rows = [x.at[PAIR * i + a] for a in range(WIN)]
    sides = [side.at[PAIR * i + a] for a in range(WIN)]
    mixer_body(rows, sides, band, filt, w_in, w_out, cot, out, gf, edge, gin, gout, gfilt, *scratch)


def place(win, at, part, side=None):
    n, cols = part.shape[:2]
    win[at : at + n, :cols, :] = part[...]
    if side is not None:
        win[at : at + n, cols:, :] = side[...]


def views(win):
    cols = win.shape[1] - TILE
    rows = [win.at[a] for a in range(WIN)]
    return rows, [win.at[a, pl.ds(cols, TILE)] for a in range(WIN)]


def beside_rows(gfilt, chans, per):
    bands, lanes = chans // per, 128
    mine = lax.broadcasted_iota(jnp.int32, (bands, chans), 1) // per == lax.broadcasted_iota(
        jnp.int32, (bands, chans), 0
    )
    lane = lax.broadcasted_iota(jnp.int32, (chans, lanes), 1)
    chan = lax.broadcasted_iota(jnp.int32, (chans, lanes), 0)
    packed = jnp.zeros((bands, lanes), F32)
    for k in range(BASIS):
        sums = jnp.sum(gfilt[8 * k : 8 * k + 8, :], axis=0, keepdims=True)
        spread = jnp.where(mine, sums, 0.0).astype(BF)
        fold = jnp.where((lane // per == k) & (lane % per == chan % per), 1.0, 0.0).astype(BF)
        packed = packed + jnp.dot(spread, fold, preferred_element_type=F32)
    row = lax.broadcasted_iota(jnp.int32, (chans, bands), 0) // per
    repeat = jnp.where(row == lax.broadcasted_iota(jnp.int32, (chans, bands), 1), 1.0, 0.0)
    return jnp.dot(repeat.astype(BF), packed.astype(BF), preferred_element_type=F32)


def outer_kernel(
    per, odd, x, side, lo, hi, band, filt, w_in, w_out, cot, partial_out, gin0, gout0, gfilt0,
    out, gf, edge, keep, give, win, gin, gout, gfilt, *scratch,
):
    i = pl.program_id(0)
    chans = gin.shape[0]

    @pl.when(i == 0)
    def _():
        gin[...] = gin0[...]
        gout[...] = gout0[...]
        gfilt[...] = gfilt0[...]
        place(win, 0, lo)
        place(win, REACH_LAT, x, side)

    @pl.when(i == 1)
    def _():
        place(win, 0, x, side)
        place(win, WIN - REACH_LAT, hi)

    rows, sides = views(win)
    mixer_body(rows, sides, band, filt, w_in, w_out, cot, out, gf, edge, gin, gout, gfilt, *scratch)

    @pl.when(i == 1)
    def _():
        beside = beside_rows(gfilt, chans, per)
        keep[:, chans:] = beside
        give[:, chans:] = beside.astype(BF)

    @pl.when((i == 1) & (odd[0] == 0))
    def _():
        keep[:, :chans] = gin[...]
        give[:, :chans] = gout[...].astype(BF)

    @pl.when((i == 1) & (odd[0] == 1))
    def _():
        keep[:, :chans] = gout[...]
        give[:, :chans] = gin[...].astype(BF)


def adjoint_body(rows, sides, band, filt, cot, out):
    cols = cot.shape[1]
    tiles = cols // TILE
    for m in range(tiles):
        full = jnp.dot(band[0], window(rows, sides, m, tiles), preferred_element_type=F32)
        at = slice(m * TILE, (m + 1) * TILE)
        for r in range(PAIR):
            total = cot[r, at, :].astype(F32)
            for k in range(BASIS):
                first = (k * PAIR + r) * TILE
                total = total + filt[k : k + 1, :] * full[first : first + TILE]
            out[r, at, :] = total.astype(BF)


def inner_adjoint(mid, mid_side, end, end_side, band, filt, cot, out, win):
    i = pl.program_id(0)

    @pl.when(i == 0)
    def _():
        place(win, 0, end, end_side)
        place(win, REACH_LAT, mid, mid_side)

    @pl.when(i == 1)
    def _():
        place(win, 0, mid, mid_side)
        place(win, WIN - REACH_LAT, end, end_side)

    adjoint_body(*views(win), band, filt, cot, out)


def outer_adjoint(mid, mid_side, end, end_side, lo, hi, band, filt, cot, partial_out, out, win):
    i = pl.program_id(0)
    place(win, REACH_LAT, end, end_side)

    @pl.when(i == 0)
    def _():
        place(win, 0, lo)
        place(win, WIN - REACH_LAT, mid, mid_side)

    @pl.when(i == 1)
    def _():
        place(win, 0, mid, mid_side)
        place(win, WIN - REACH_LAT, hi)

    adjoint_body(*views(win), band, filt, cot, out)


def blocks(n, shape, step=None):
    step = step or (lambda i: i)
    return pl.BlockSpec((n,) + shape[1:], lambda i: (step(i),) + (0,) * (len(shape) - 1))


def whole(shape):
    return pl.BlockSpec(shape, lambda i: (0,) * len(shape))


def params(limit=VMEM_LIMIT):
    return pltpu.CompilerParams(vmem_limit_bytes=limit)


def mixer_scratch(cols, chans):
    cells = PAIR * cols
    return [
        pltpu.VMEM((BASIS, cells, chans), F32),
        pltpu.VMEM((cells, chans), BF),
        pltpu.VMEM((cells, chans), F32),
        pltpu.VMEM((cells, chans), F32),
        pltpu.VMEM((cells, chans), BF),
        pltpu.VMEM((cells, chans), BF),
    ]


def mixer_cost(cols, chans):
    cells = 2 * PAIR * cols
    flops = 2 * cells * chans * (6 * chans + BASIS * WIN * SPAN)
    return pl.CostEstimate(
        flops=flops, bytes_accessed=10 * cells * chans, transcendentals=cells * chans
    )


def inner_pair(i):
    return 1 + i


def outer_pair(i):
    return 3 * i


def mixer_inner(x, side, band, filt, w_in, w_out, cot):
    rows, cols, chans = x.shape
    gf = jax.ShapeDtypeStruct((2 * PAIR, cols, chans), BF)
    edge = jax.ShapeDtypeStruct((2 * PAIR, TILE, chans), BF)
    matrix = jax.ShapeDtypeStruct((chans, chans), F32)
    small = jax.ShapeDtypeStruct((8 * BASIS, chans), F32)
    return pl.pallas_call(
        inner_kernel,
        grid=(2,),
        in_specs=[
            whole(x.shape), whole(side.shape), blocks(1, band.shape, inner_pair),
            whole(filt.shape), whole(w_in.shape), whole(w_out.shape),
            blocks(PAIR, cot.shape, inner_pair),
        ],
        out_specs=[
            blocks(PAIR, x.shape, inner_pair), blocks(PAIR, gf.shape), blocks(PAIR, edge.shape),
            whole(matrix.shape), whole(matrix.shape), whole(small.shape),
        ],
        out_shape=(jax.ShapeDtypeStruct(x.shape, BF), gf, edge, matrix, matrix, small),
        scratch_shapes=mixer_scratch(cols, chans),
        compiler_params=params(),
        cost_estimate=mixer_cost(cols, chans),
        name="mixer_inner",
    )(x, side, band, filt, w_in, w_out, cot)


def mixer_outer(
    odd, per, x, side, lo, hi, band, filt, w_in, w_out, cot, partial_out, sums
):
    rows, cols, chans = x.shape
    near = WIN - REACH_LAT
    gf = jax.ShapeDtypeStruct((2 * PAIR, cols, chans), BF)
    edge = jax.ShapeDtypeStruct((2 * PAIR, TILE, chans), BF)
    keep = jax.ShapeDtypeStruct((chans, chans + 128), F32)
    give = jax.ShapeDtypeStruct((chans, chans + 128), BF)
    return pl.pallas_call(
        functools.partial(outer_kernel, per),
        grid=(2,),
        in_specs=[
            pl.BlockSpec(memory_space=pltpu.SMEM),
            blocks(near, x.shape), blocks(near, side.shape),
            whole(lo.shape), whole(hi.shape),
            blocks(1, band.shape, outer_pair),
            whole(filt.shape), whole(w_in.shape), whole(w_out.shape),
            blocks(PAIR, cot.shape, outer_pair),
            pl.BlockSpec(memory_space=pl.ANY),
        ] + [whole(s.shape) for s in sums],
        out_specs=[
            blocks(PAIR, x.shape, outer_pair), blocks(PAIR, gf.shape), blocks(PAIR, edge.shape),
            whole(keep.shape), whole(give.shape),
        ],
        out_shape=(jax.ShapeDtypeStruct(x.shape, BF), gf, edge, keep, give),
        scratch_shapes=[
            pltpu.VMEM((WIN, cols + TILE, chans), BF),
            pltpu.VMEM((chans, chans), F32),
            pltpu.VMEM((chans, chans), F32),
            pltpu.VMEM((8 * BASIS, chans), F32),
        ] + mixer_scratch(cols, chans),
        input_output_aliases={10: 0},
        compiler_params=params(),
        cost_estimate=mixer_cost(cols, chans),
        name="mixer_outer",
    )(odd, x, side, lo, hi, band, filt, w_in, w_out, cot, partial_out, *sums)


def adjoint_cost(cols, chans):
    cells = 2 * PAIR * cols
    return pl.CostEstimate(
        flops=2 * cells * chans * BASIS * WIN * SPAN, bytes_accessed=6 * cells * chans,
        transcendentals=0,
    )


def adjoint_inner(mid, mid_side, end, end_side, band, filt, cot):
    rows, cols, chans = cot.shape
    return pl.pallas_call(
        inner_adjoint,
        grid=(2,),
        in_specs=[
            whole(mid.shape), whole(mid_side.shape),
            blocks(PAIR, end.shape), blocks(PAIR, end_side.shape),
            blocks(1, band.shape, inner_pair), whole(filt.shape),
            blocks(PAIR, cot.shape, inner_pair),
        ],
        out_specs=blocks(PAIR, cot.shape, inner_pair),
        out_shape=jax.ShapeDtypeStruct(cot.shape, BF),
        scratch_shapes=[pltpu.VMEM((WIN, cols + TILE, chans), BF)],
        compiler_params=params(SMALL_LIMIT),
        cost_estimate=adjoint_cost(cols, chans),
        name="adjoint_inner",
    )(mid, mid_side, end, end_side, band, filt, cot)


def adjoint_outer(mid, mid_side, end, end_side, lo, hi, band, filt, cot, partial_out):
    rows, cols, chans = cot.shape
    return pl.pallas_call(
        outer_adjoint,
        grid=(2,),
        in_specs=[
            blocks(PAIR, mid.shape), blocks(PAIR, mid_side.shape),
            blocks(PAIR, end.shape), blocks(PAIR, end_side.shape),
            whole(lo.shape), whole(hi.shape),
            blocks(1, band.shape, outer_pair), whole(filt.shape),
            blocks(PAIR, cot.shape, outer_pair),
            pl.BlockSpec(memory_space=pl.ANY),
        ],
        out_specs=blocks(PAIR, cot.shape, outer_pair),
        out_shape=jax.ShapeDtypeStruct(cot.shape, BF),
        scratch_shapes=[pltpu.VMEM((WIN, cols + TILE, chans), BF)],
        input_output_aliases={9: 0},
        compiler_params=params(),
        cost_estimate=adjoint_cost(cols, chans),
        name="adjoint_outer",
    )(mid, mid_side, end, end_side, lo, hi, band, filt, cot, partial_out)


def exchange_columns(first, last, count):
    up = [(i, (i + 1) % count) for i in range(count)]
    down = [(i, (i - 1) % count) for i in range(count)]
    right = lax.ppermute(first, "lon", down)
    left = lax.ppermute(last, "lon", up)
    return jnp.concatenate([right, left], axis=1)


def beside(rows, side):
    return jnp.concatenate([rows, side], axis=1)


def exchange_rows(first, last, count):
    up = [(i, i + 1) for i in range(count - 1)]
    down = [(i + 1, i) for i in range(count - 1)]
    return lax.ppermute(last, "lat", up), lax.ppermute(first, "lat", down)


def swap(a, count, bits):
    return lax.ppermute(a, "lon", [(i, i ^ bits) for i in range(count)])


def sum_kernel(chans, filters, copies, spread, share, square):
    total = jnp.sum(spread[...].astype(F32), axis=0)
    share[...] = total
    sq = total * total
    lane = lax.broadcasted_iota(jnp.int32, sq.shape, 1)
    row = lax.broadcasted_iota(jnp.int32, sq.shape, 0)
    beside = jnp.where((row == 0) & (lane < chans + filters), sq / copies, 0.0)
    square[...] = jnp.full(square.shape, jnp.sum(jnp.where(lane < chans, sq, beside)), F32)


def sum_shares(spread, chans, filters, copies):
    return pl.pallas_call(
        functools.partial(sum_kernel, chans, filters, copies),
        out_shape=(
            jax.ShapeDtypeStruct(spread.shape[1:], F32),
            jax.ShapeDtypeStruct((1, 128), F32),
        ),
        compiler_params=params(SMALL_LIMIT),
        name="sum_shares",
    )(spread)


def scale_kernel(per, flags, every, mats, near, across, far, beside, w_in, w_out, filters, work):
    total = jnp.sum(every[...], axis=0)
    scale = jnp.minimum(1.0, CLIP / jnp.sqrt(total + EPS))[:, :1]
    half = mats.shape[0]
    upper = jnp.full(mats.shape, flags[1], jnp.int32) == 1
    for n, (own, other) in enumerate(((mats, near), (across, far))):
        work[n, :half, :] = jnp.where(upper, other[...], own[...]) * scale
        work[n, half:, :] = jnp.where(upper, own[...], other[...]) * scale
    odd = jnp.full(w_in.shape, flags[0], jnp.int32) == 1
    w_in[...] = jnp.where(odd, work[1], work[0])
    w_out[...] = jnp.where(odd, work[0], work[1]).T
    lanes = beside.shape[1]
    lane = lax.broadcasted_iota(jnp.int32, (per, lanes), 1)
    chan = lax.broadcasted_iota(jnp.int32, (per, lanes), 0)
    spread = jnp.where(lane % per == chan, beside[...], 0.0)
    at = lax.broadcasted_iota(jnp.int32, (lanes, BASIS), 0) // per
    fold = jnp.where(at == lax.broadcasted_iota(jnp.int32, (lanes, BASIS), 1), 1.0, 0.0)
    sums = jnp.dot(spread, fold, precision=lax.Precision.HIGHEST, preferred_element_type=F32)
    filters[...] = sums * scale


def scaled(flags, every, mats, near, across, far, beside, per):
    chans = mats.shape[1]
    blocks_in = [pl.BlockSpec(memory_space=pltpu.SMEM)]
    blocks_in += [pl.BlockSpec(memory_space=pltpu.VMEM)] * 6
    return pl.pallas_call(
        functools.partial(scale_kernel, per),
        in_specs=blocks_in,
        out_shape=(
            jax.ShapeDtypeStruct((per, chans), F32),
            jax.ShapeDtypeStruct((chans, per), F32),
            jax.ShapeDtypeStruct((per, BASIS), F32),
        ),
        scratch_shapes=[pltpu.VMEM((2, per, chans), F32)],
        compiler_params=params(SMALL_LIMIT),
        name="scaled",
    )(flags, every, mats, near, across, far, beside)


def local(
    bands, panels,
    inputs, cotangent, basis_values, basis_index, lon_reach, filters, weight_in, weight_out,
):
    rows, cols, chans = inputs.shape
    pairs = rows // PAIR
    per = chans // bands
    first_row = lax.axis_index("lat") * rows
    ext = rows + 2 * REACH_LAT
    with jax.named_scope("input_halo"):
        side = exchange_columns(inputs[:, :HALF], inputs[:, cols - HALF :], panels)
        lo, hi = exchange_rows(
            beside(inputs[:REACH_LAT], side[:REACH_LAT]),
            beside(inputs[rows - REACH_LAT :], side[rows - REACH_LAT :]), bands,
        )
    with jax.named_scope("bands"):

        def cut(a):
            padded = jnp.pad(a, ((REACH_LAT, REACH_LAT),) + ((0, 0),) * (a.ndim - 1))
            return lax.dynamic_slice_in_dim(padded, first_row, ext, 0)

        tables = (
            cut(basis_values).reshape(-1, COL_TAPS).T,
            cut(basis_index).reshape(-1, COL_TAPS).T,
            cut(lon_reach).reshape(1, -1),
        )
        band = band_matrix(0, *tables, pairs)
        filt = filters.T
    out, gf_mid, edge_mid, *sums = mixer_inner(
        inputs, side, band, filt, weight_in, weight_out, cotangent
    )
    tables, out = lax.optimization_barrier((tables, out))
    band_adj = band_matrix(1, *tables, pairs)
    core = lax.axis_index("lon") % 2
    out, gf_end, edge_end, keep, give = mixer_outer(
        core.astype(jnp.int32).reshape(1), per, inputs, side, lo, hi, band, filt,
        weight_in, weight_out, cotangent, out, sums,
    )
    with jax.named_scope("grad_halo"):
        edge = jnp.concatenate([edge_end, edge_mid], axis=0)
        gside = exchange_columns(edge[:, :HALF], edge[:, HALF:], panels)
        end_side, mid_side = gside[: 2 * PAIR], gside[2 * PAIR :]
        ends = beside(gf_end[:PAIR], end_side[:PAIR]), beside(gf_end[PAIR:], end_side[PAIR:])
    with jax.named_scope("reduce"):
        lanes, half = chans + 128, per // 2
        total = (keep + swap(give, panels, 1).astype(F32)).reshape(bands, per, lanes)
        upper = lax.axis_index("lon") // 2 == 1
        kept = jnp.where(upper, total[:, half:], total[:, :half])
        give = jnp.where(upper, total[:, :half], total[:, half:]).astype(BF)
        part = (kept + swap(give, panels, 2).astype(F32)).astype(BF)
        part, ends = lax.optimization_barrier((part, ends))
        halos = exchange_rows(*ends, bands)
        spread = lax.all_to_all(part, "lat", 0, 0)
        halos, gf_mid = lax.optimization_barrier((halos, gf_mid))
        back = adjoint_inner(gf_mid, mid_side, gf_end, end_side, band_adj, filt, cotangent)
        spread, back = lax.optimization_barrier((spread, back))
    with jax.named_scope("norm"):
        share, square = sum_shares(spread, chans, BASIS * per, panels)
        mats = share[:, :chans]
        near, across, far = (swap(mats, panels, bits) for bits in (2, 1, 3))
        every = lax.all_to_all(
            jnp.broadcast_to(square, (bands * panels, 1, 128)), ("lat", "lon"), 0, 0
        )
        near, across, far, every = lax.optimization_barrier((near, across, far, every))
        flags = jnp.stack([core, lax.axis_index("lon") // 2]).astype(jnp.int32)
        shares = scaled(flags, every, mats, near, across, far, share[:1, chans:], per)
    back = adjoint_outer(
        gf_mid, mid_side, gf_end, end_side, *halos, band_adj, filt, cotangent, back
    )
    return (out, back, *shares)


def solution(mesh):
    bands, panels = mesh.shape["lat"], mesh.shape["lon"]
    field = P("lat", "lon", None)
    return jax.shard_map(
        functools.partial(local, bands, panels),
        mesh=mesh,
        in_specs=(field, field, P(), P(), P(), P(), P(), P()),
        out_specs=(field, field, P("lat", None), P(None, "lat"), P("lat", None)),
        check_vma=False,
    )
```
